32 devices in a mesh: row: 8 (over z, core), col: 4 (over y, x).
Axes of the slice: x: 2, y: 2, z: 4, core: 2. Of those that a mesh axis runs over, the one named last changes fastest.
Arguments:
- values: bfloat16 [16, 8, 128, 128], P('row', 'col'), as said below
- columns: int32 [16, 8], P('row', 'col'), may hold values from 0 to 15, as said below
Outputs:
- sign_blocks: float32 [16, 8, 128, 128], P('row', 'col')
The draws below stay inside these ranges and needn't reach their ends.
Inputs may be any that keep to these rules, and one draw needn't show every extreme that they name: Block row i keeps 2 distinct block columns in each panel of 4 consecutive block columns, slot s lying in panel s // 2; slot (i // 4) * 2 of row i is its diagonal block; the pattern is symmetric: j is kept in row i exactly when i is kept in row j. `values`: the blocks are those of a symmetric matrix.
All inputs are finite; a program needn't handle non-finite values.
Results may differ from the reference program's by a relative error of at most 0.003.
Values may be sent and summed in bfloat16 or wider, within the bound.
No kernel may reach another device: no remote copies, remote signals or barrier semaphores. Data moves between devices by JAX's collectives and lax.ppermute only.
A program may use at most 64 MiB of HBM per device.

```python
import jax
import jax.numpy as jnp
from jax import lax

BS = 128
SLOTS = 2
ITERS = 1
NB = 16
PANEL = 4
KEPT = 8
ORDER = 2048


def pattern_from(key):
    panels = NB // PANEL
    several = jax.random.split(key, panels * panels)
    shuffles = jax.vmap(lambda single: jax.random.permutation(single, PANEL))(several)
    shuffles = shuffles.reshape(panels, panels, PANEL).astype(jnp.int32)
    inverse = jnp.argsort(shuffles, axis=-1).astype(jnp.int32)
    block_rows = jnp.arange(NB, dtype=jnp.int32)
    home = block_rows // PANEL
    within = block_rows % PANEL
    panel_ids = jnp.arange(panels, dtype=jnp.int32)
    offset = jnp.arange(SLOTS, dtype=jnp.int32)
    forward = shuffles[home[:, None], panel_ids[None, :], within[:, None]]
    upper = (forward[:, :, None] + offset[None, None, :]) % PANEL
    back_index = (within[:, None, None] - offset[None, None, :]) % PANEL
    lower = inverse[panel_ids[None, :, None], home[:, None, None], back_index]
    diagonal = (within[:, None, None] + offset[None, None, :] * (PANEL // 2)) % PANEL
    diagonal = jnp.broadcast_to(diagonal, upper.shape)
    above = home[:, None, None] < panel_ids[None, :, None]
    below = home[:, None, None] > panel_ids[None, :, None]
    chosen = jnp.where(above, upper, jnp.where(below, lower, diagonal))
    result = panel_ids[None, :, None] * PANEL + chosen
    return result.reshape(NB, KEPT).astype(jnp.int32)


def draw_columns(key, part):
    return pattern_from(key)


def draw_values(key, part):
    pattern = pattern_from(key)
    key = jax.random.fold_in(key, 5)
    first, second = jax.random.split(key)
    spread = 0.5 / (BS * KEPT) ** 0.5
    noise = jax.random.normal(first, (ORDER, ORDER), jnp.float32)
    shift = jax.random.uniform(second, (NB, BS), jnp.float32, -0.4, 0.4)
    symmetric = (noise + noise.T) * 0.5 ** 0.5 * spread
    tiled = symmetric.reshape(NB, BS, NB, BS).transpose(0, 2, 1, 3)
    blocks = jnp.take_along_axis(tiled, pattern[:, :, None, None], axis=1)
    on_diagonal = (pattern == jnp.arange(NB, dtype=jnp.int32)[:, None]).astype(jnp.float32)
    shifted = shift[:, :, None] * jnp.eye(BS, dtype=jnp.float32)[None, :, :]
    blocks = blocks + on_diagonal[:, :, None, None] * shifted[:, None, :, :]
    return blocks.astype(jnp.bfloat16)


def setup_inputs(seed: int = 0) -> dict:
    key_list = jax.random.split(jax.random.key(seed), 3)
    values = draw_values(jax.random.fold_in(key_list[2], 71), 0)
    columns = draw_columns(jax.random.fold_in(key_list[2], 71), 0)
    return {"values": values, "columns": columns}


def select_blocks(right, columns, row_columns):
    partner = columns[row_columns]
    width = partner.shape[1]
    match = partner[:, :, None] == row_columns[None, None, :]
    found = jnp.any(match, axis=1)
    where_slot = jnp.sum(jnp.where(match, jnp.arange(width, dtype=jnp.int32)[None, :, None], 0), axis=1).astype(jnp.int32)
    picked = right[row_columns[:, None], where_slot].astype(jnp.float32)
    return jnp.where(found[:, :, None, None], picked, jnp.zeros((), jnp.float32))


def restricted_product(left, right, columns):
    def one_row(item):
        row_blocks, row_columns = item
        picked = select_blocks(right, columns, row_columns)
        return jnp.einsum('sxz,stzy->txy', row_blocks.astype(jnp.float32), picked, precision=lax.Precision.HIGHEST)
    return lax.map(one_row, (left, columns))


def reference(values, columns):
    block_rows = jnp.arange(values.shape[0], dtype=jnp.int32)
    on_diagonal = (columns == block_rows[:, None]).astype(jnp.float32)
    identity = on_diagonal[:, :, None, None] * jnp.eye(BS, dtype=jnp.float32)[None, None, :, :]
    current = values
    updated = values.astype(jnp.float32)
    for step in range(ITERS):
        square = restricted_product(current, current, columns)
        square_low = square.astype(jnp.bfloat16)
        fourth = restricted_product(square_low, square_low, columns)
        polynomial = (15.0 * identity - 10.0 * square_low.astype(jnp.float32) + 3.0 * fourth).astype(jnp.bfloat16)
        updated = restricted_product(current, polynomial, columns) * 0.125
        current = updated.astype(jnp.bfloat16)
    return updated
```

```python
import functools

import jax
import jax.numpy as jnp
from jax import lax
from jax.experimental import pallas as pl
from jax.experimental.pallas import tpu as pltpu
from jax.sharding import PartitionSpec as P

REPLICA_LIMIT = 8 * 1024 * 1024


def select_blocks(panel_blocks, panel_slots, row_columns, targets):
    partner = jnp.take(panel_slots, row_columns, axis=0)
    width = partner.shape[2]
    match = partner[:, :, :, None] == targets[:, None, None, :]
    found = jnp.any(match, axis=2)
    where_slot = jnp.sum(
        jnp.where(match, jnp.arange(width, dtype=jnp.int32)[None, None, :, None], 0), axis=2
    )
    picked = panel_blocks[row_columns[:, :, None], where_slot]
    return jnp.where(found[:, :, :, None, None], picked, jnp.zeros((), picked.dtype))


def partial_product(row_blocks, row_columns, panel_blocks, panel_slots, targets):
    picked = select_blocks(panel_blocks, panel_slots, row_columns, targets)
    return jnp.einsum("bsxz,bstzy->btxy", row_blocks, picked, preferred_element_type=jnp.float32)


def gather_panel(blocks):
    return lax.all_gather(blocks, "row", axis=0, tiled=True)


def per_device_panels(values, columns):
    rows_here, slots_here, block = (values.shape[0], values.shape[1], values.shape[2])
    row_ids = lax.axis_index("row") * rows_here + jnp.arange(rows_here, dtype=jnp.int32)
    on_diagonal = (columns == row_ids[:, None]).astype(jnp.float32)
    identity = on_diagonal[:, :, None, None] * jnp.eye(block, dtype=jnp.float32)[None, None, :, :]
    panel_blocks = lax.all_gather(values, "row", axis=0, tiled=True)
    panel_slots = lax.all_gather(columns, "row", axis=0, tiled=True)
    row_blocks = lax.all_gather(values, "col", axis=1, tiled=True)
    row_columns = lax.all_gather(columns, "col", axis=1, tiled=True)
    square = partial_product(row_blocks, row_columns, panel_blocks, panel_slots, columns)
    square_low = square.astype(jnp.bfloat16)
    square_panel = gather_panel(square_low)
    square_rows = lax.all_gather(square_low, "col", axis=1, tiled=True)
    fourth = partial_product(square_rows, row_columns, square_panel, panel_slots, columns)
    polynomial = (15.0 * identity - 10.0 * square_low.astype(jnp.float32) + 3.0 * fourth).astype(
        jnp.bfloat16
    )
    polynomial_panel = gather_panel(polynomial)
    updated = (
        partial_product(row_blocks, row_columns, polynomial_panel, panel_slots, columns) * 0.125
    )
    return updated


def local_iteration(
    rows, kept, rows_here, slots_here, place, columns, origin, blocks, out, xs, ys, qs, table, sem
):
    count = rows * kept
    size = xs.shape[1]
    copy = pltpu.make_async_copy(blocks, xs.at[pl.ds(0, count)], sem)
    copy.start()

    def clear(at, carry):
        table[at] = count
        return carry

    def enter(at, carry):
        table[lax.div(at, kept) * rows + columns[at]] = at
        return carry

    lax.fori_loop(0, rows * rows, clear, 0, unroll=8)
    lax.fori_loop(0, count, enter, 0, unroll=8)
    nothing = jnp.zeros((size, size), jnp.bfloat16)
    xs[count] = nothing
    ys[count] = nothing
    qs[rows * slots_here] = nothing
    row_here, panel = origin[0], origin[1]
    copy.wait()

    def wide(parts):
        return jnp.concatenate(parts, axis=1)

    def tall(parts):
        return jnp.concatenate(parts, axis=0)

    def dot(left, right):
        return jnp.dot(left, right, preferred_element_type=jnp.float32)

    def square(i, carry):
        ks = [columns[i * kept + s] for s in range(kept)]
        left = wide([xs[place(i * kept + s)] for s in range(kept)])
        for first in range(0, kept, slots_here):
            right = tall(
                [
                    wide(
                        [xs[place(table[k * rows + ks[first + t]])] for t in range(slots_here)]
                    )
                    for k in ks
                ]
            )
            product = dot(left, right).astype(jnp.bfloat16)
            for t in range(slots_here):
                ys[i * kept + first + t] = product[:, t * size : (t + 1) * size]
        return carry

    lax.fori_loop(0, rows, square, 0)

    eye = (
        lax.broadcasted_iota(jnp.int32, (size, size), 0)
        == lax.broadcasted_iota(jnp.int32, (size, size), 1)
    ).astype(jnp.float32)

    def polynomial(i, carry):
        ks = [columns[i * kept + s] for s in range(kept)]
        first = i * kept + panel * slots_here
        js = [columns[first + t] for t in range(slots_here)]
        left = wide([ys[i * kept + s] for s in range(kept)])
        right = tall([wide([ys[table[k * rows + j]] for j in js]) for k in ks])
        fourth = dot(left, right)
        for t in range(slots_here):
            scale = jnp.where(js[t] == i, 15.0, 0.0)
            low = ys[first + t].astype(jnp.float32)
            value = scale * eye - 10.0 * low + 3.0 * fourth[:, t * size : (t + 1) * size]
            qs[i * slots_here + t] = value.astype(jnp.bfloat16)
        return carry

    lax.fori_loop(0, rows, polynomial, 0)

    for a in range(rows_here):
        i = row_here + a
        ks = [columns[i * kept + s] for s in range(kept)]
        js = [columns[i * kept + panel * slots_here + t] for t in range(slots_here)]

        def entry(k, j):
            at = table[k * rows + j]
            inside = k * slots_here + lax.rem(at, slots_here)
            return jnp.where(at == count, rows * slots_here, inside)

        left = wide([xs[place(i * kept + s)] for s in range(kept)])
        right = tall([wide([qs[entry(k, j)] for j in js]) for k in ks])
        updated = dot(left, right) * 0.125
        for t in range(slots_here):
            out[a, t] = updated[:, t * size : (t + 1) * size]


def per_device_whole(values, columns):
    rows_here, slots_here, size = values.shape[0], values.shape[1], values.shape[2]
    panels = lax.axis_size("col")
    rows = rows_here * lax.axis_size("row")
    kept = slots_here * panels
    blocks = lax.all_gather(values, ("row", "col"), axis=0, tiled=True)
    blocks = blocks.reshape(rows * kept, size, size)
    slots = lax.all_gather(columns, ("row", "col"), axis=0, tiled=False)
    slots = slots.reshape(rows // rows_here, panels, rows_here, slots_here)
    slots = slots.transpose(0, 2, 1, 3).reshape(rows * kept)
    origin = jnp.stack([lax.axis_index("row") * rows_here, lax.axis_index("col")])

    def place(at):
        i, s = lax.div(at, kept), lax.rem(at, kept)
        band = lax.div(i, rows_here) * panels + lax.div(s, slots_here)
        return (band * rows_here + lax.rem(i, rows_here)) * slots_here + lax.rem(s, slots_here)

    count = rows * kept
    return pl.pallas_call(
        functools.partial(local_iteration, rows, kept, rows_here, slots_here, place),
        out_shape=jax.ShapeDtypeStruct(values.shape, jnp.float32),
        in_specs=[
            pl.BlockSpec(memory_space=pltpu.SMEM),
            pl.BlockSpec(memory_space=pltpu.SMEM),
            pl.BlockSpec(memory_space=pl.ANY),
        ],
        out_specs=pl.BlockSpec(memory_space=pltpu.VMEM),
        scratch_shapes=[
            pltpu.VMEM((count + 1, size, size), jnp.bfloat16),
            pltpu.VMEM((count + 1, size, size), jnp.bfloat16),
            pltpu.VMEM((rows * slots_here + 1, size, size), jnp.bfloat16),
            pltpu.SMEM((rows * rows,), jnp.int32),
            pltpu.SemaphoreType.DMA,
        ],
        compiler_params=pltpu.CompilerParams(vmem_limit_bytes=32 * 1024 * 1024),
    )(slots, origin.astype(jnp.int32), blocks)


def per_device(values, columns):
    devices = lax.axis_size("row") * lax.axis_size("col")
    whole = devices * values.size * values.dtype.itemsize
    if whole <= REPLICA_LIMIT:
        return per_device_whole(values, columns)
    return per_device_panels(values, columns)


def solution(mesh):
    in_specs = (P("row", "col", None, None), P("row", "col"))
    out_specs = P("row", "col", None, None)
    return jax.shard_map(
        per_device, mesh=mesh, in_specs=in_specs, out_specs=out_specs, check_vma=False
    )
```

```python
import functools

import jax
import jax.numpy as jnp
from jax import lax
from jax.experimental import pallas as pl
from jax.experimental.pallas import tpu as pltpu
from jax.sharding import PartitionSpec as P

def select_blocks(panel_blocks, panel_slots, row_columns, targets):
    partner = jnp.take(panel_slots, row_columns, axis=0)
    width = partner.shape[2]
    match = partner[:, :, :, None] == targets[:, None, None, :]
    found = jnp.any(match, axis=2)
    where_slot = jnp.sum(
        jnp.where(match, jnp.arange(width, dtype=jnp.int32)[None, None, :, None], 0), axis=2
    )
    picked = panel_blocks[row_columns[:, :, None], where_slot]
    return jnp.where(found[:, :, :, None, None], picked, jnp.zeros((), picked.dtype))


def partial_product(row_blocks, row_columns, panel_blocks, panel_slots, targets):
    picked = select_blocks(panel_blocks, panel_slots, row_columns, targets)
    return jnp.einsum("bsxz,bstzy->btxy", row_blocks, picked, preferred_element_type=jnp.float32)


def gather_panel(blocks):
    return lax.all_gather(blocks, "row", axis=0, tiled=True)


def per_device_panels(values, columns):
    rows_here, slots_here, block = (values.shape[0], values.shape[1], values.shape[2])
    row_ids = lax.axis_index("row") * rows_here + jnp.arange(rows_here, dtype=jnp.int32)
    on_diagonal = (columns == row_ids[:, None]).astype(jnp.float32)
    identity = on_diagonal[:, :, None, None] * jnp.eye(block, dtype=jnp.float32)[None, None, :, :]
    panel_blocks = lax.all_gather(values, "row", axis=0, tiled=True)
    panel_slots = lax.all_gather(columns, "row", axis=0, tiled=True)
    row_blocks = lax.all_gather(values, "col", axis=1, tiled=True)
    row_columns = lax.all_gather(columns, "col", axis=1, tiled=True)
    square = partial_product(row_blocks, row_columns, panel_blocks, panel_slots, columns)
    square_low = square.astype(jnp.bfloat16)
    square_panel = gather_panel(square_low)
    square_rows = lax.all_gather(square_low, "col", axis=1, tiled=True)
    fourth = partial_product(square_rows, row_columns, square_panel, panel_slots, columns)
    polynomial = (15.0 * identity - 10.0 * square_low.astype(jnp.float32) + 3.0 * fourth).astype(
        jnp.bfloat16
    )
    polynomial_panel = gather_panel(polynomial)
    updated = (
        partial_product(row_blocks, row_columns, polynomial_panel, panel_slots, columns) * 0.125
    )
    return updated


def local_iteration(
    parts, rows, kept, rows_here, slots_here, left_at, square_at, fourth_at, update_at, origin, *rest
):
    blocks, (out, xs, ys, qs, sem) = rest[:-5], rest[-5:]
    per_piece, size = rows_here * slots_here, xs.shape[1]
    core = origin[2]
    copies = []
    for block, (piece, sibling_part) in zip(blocks, parts):
        side = 1 - core if sibling_part else core
        for step in range(block.shape[0] // per_piece):
            copies.append(
                pltpu.make_async_copy(
                    block.at[pl.ds(step * per_piece, per_piece)],
                    xs.at[pl.ds(((piece + step) * 2 + side) * per_piece, per_piece)],
                    sem.at[len(copies)],
                )
            )
    for copy in copies:
        copy.start()
    received = 10 * 2 * per_piece
    nothing = jnp.zeros((size, size), jnp.bfloat16)
    xs[xs.shape[0] - 1] = nothing
    ys[rows * kept] = nothing
    qs[rows * slots_here] = nothing
    row_here, panel = origin[0], origin[1]
    for copy in copies:
        copy.wait()

    for number, piece in enumerate((0, 1, 2, 3, 5, 7, 9)):
        for inside in range(2 * per_piece):
            xs[received + number * 2 * per_piece + inside] = xs[
                piece * 2 * per_piece + inside
            ].T

    def wide(parts):
        return jnp.concatenate(parts, axis=1)

    def tall(parts):
        return jnp.concatenate(parts, axis=0)

    def dot(left, right):
        return jnp.dot(left, right, preferred_element_type=jnp.float32)

    def square(i, carry):
        left = wide([xs[left_at[i * kept + s]] for s in range(kept)])
        for first in range(0, kept, slots_here):
            right = tall(
                [
                    wide(
                        [
                            xs[square_at[(i * kept + s) * kept + first + t]]
                            for t in range(slots_here)
                        ]
                    )
                    for s in range(kept)
                ]
            )
            product = dot(left, right).astype(jnp.bfloat16)
            for t in range(slots_here):
                ys[i * kept + first + t] = product[:, t * size : (t + 1) * size]
        return carry

    lax.fori_loop(0, rows, square, 0)

    eye = (
        lax.broadcasted_iota(jnp.int32, (size, size), 0)
        == lax.broadcasted_iota(jnp.int32, (size, size), 1)
    ).astype(jnp.float32)

    def polynomial(i, carry):
        first = i * kept + panel * slots_here
        left = wide([ys[i * kept + s] for s in range(kept)])
        right = tall(
            [
                wide(
                    [ys[fourth_at[(i * kept + s) * slots_here + t]] for t in range(slots_here)]
                )
                for s in range(kept)
            ]
        )
        fourth = dot(left, right)
        for t in range(slots_here):
            scale = origin[3 + i * slots_here + t].astype(jnp.float32)
            low = ys[first + t].astype(jnp.float32)
            value = scale * eye - 10.0 * low + 3.0 * fourth[:, t * size : (t + 1) * size]
            qs[i * slots_here + t] = value.astype(jnp.bfloat16)
        return carry

    lax.fori_loop(0, rows, polynomial, 0)

    for a in range(rows_here):
        i = row_here + a
        left = wide([xs[left_at[i * kept + s]] for s in range(kept)])
        right = tall(
            [
                wide(
                    [qs[update_at[(i * kept + s) * slots_here + t]] for t in range(slots_here)]
                )
                for s in range(kept)
            ]
        )
        updated = dot(left, right) * 0.125
        for t in range(slots_here):
            out[a, t] = updated[:, t * size : (t + 1) * size]


NEXT = (0, 2, 3, 1)


def around(array, step, bands):
    return lax.ppermute(array, "row", [(r, (r + 2 * step) % bands) for r in range(bands)])


def across(array, flip):
    return lax.ppermute(array, "col", [(c, c ^ flip) for c in range(4)])


def sibling(array, bands):
    return lax.ppermute(array, "row", [(r, r ^ 1) for r in range(bands)])


def all_columns(columns, bands, z, c, core):
    other = sibling(columns, bands)
    lower = jnp.where(core == 0, columns, other)
    upper = jnp.where(core == 0, other, columns)
    mine = jnp.concatenate([lower, upper], axis=0)
    line = [mine] + [around(mine, step, bands) for step in range(1, 4)]
    line = jnp.stack(line)
    line = line[(z - jnp.arange(4)) % 4]
    line = line.reshape(4 * mine.shape[0], mine.shape[1])
    plane = jnp.stack([line] + [across(line, flip) for flip in range(1, 4)])
    plane = plane[c ^ jnp.arange(4)]
    return plane.transpose(1, 0, 2).reshape(line.shape[0], -1)


def address_tables(pattern, z, c, slots_here, per_chip):
    rows, kept = pattern.shape
    ids = jnp.arange(rows, dtype=jnp.int32)
    match = pattern[:, :, None] == ids[None, None, :]
    found = jnp.any(match, axis=1)
    slot = jnp.sum(jnp.where(match, jnp.arange(kept, dtype=jnp.int32)[None, :, None], 0), axis=1)
    natural = jnp.where(found, ids[:, None] * kept + slot, rows * kept)
    half = slot % slots_here
    inside = (ids[:, None] % 4) * slots_here + half
    inside_t = inside.T
    h = (ids // 4)[:, None]
    g = (ids // 4)[None, :]
    received, mirror = 10 * per_chip, 10 * per_chip + 4 * per_chip
    own = ((z - h) % 4) * per_chip + inside
    own_mirror = received + ((z - g) % 4) * per_chip + inside_t
    flip_g, flip_h = g ^ c, h ^ c
    diagonal = (4 + (flip_g - 1) * 2) * per_chip + inside
    turn = jnp.array(NEXT, jnp.int32)
    pair = (5 + (flip_g - 1) * 2) * per_chip + inside
    pair_mirror = mirror + (flip_h - 1) * per_chip + inside_t
    place = jnp.where(turn[flip_g] == (h ^ g), pair, pair_mirror)
    place = jnp.where(h == g, diagonal, place)
    place = jnp.where(h == c, own_mirror, place)
    place = jnp.where(g == c, own, place)
    place = jnp.where(found, place, mirror + 3 * per_chip)
    in_panel = lax.dynamic_slice_in_dim(pattern, c * slots_here, slots_here, axis=1)
    left_at = place[ids[:, None], pattern]
    square_at = place[pattern[:, :, None], pattern[:, None, :]]
    fourth_at = natural[pattern[:, :, None], in_panel[:, None, :]]
    panel_at = jnp.where(found, ids[:, None] * slots_here + half, rows * slots_here)
    update_at = panel_at[pattern[:, :, None], in_panel[:, None, :]]
    on_diagonal = jnp.where(in_panel == ids[:, None], 15, 0)
    return left_at, square_at, fourth_at, update_at, on_diagonal


def per_device_whole(values, columns):
    rows_here, slots_here, size = values.shape[0], values.shape[1], values.shape[2]
    bands, panels = lax.axis_size("row"), lax.axis_size("col")
    rows, kept = rows_here * bands, slots_here * panels
    per_piece = rows_here * slots_here
    band, c = lax.axis_index("row"), lax.axis_index("col")
    z, core = band // 2, band % 2
    mine = values.reshape(per_piece, size, size)
    line = [mine] + [around(mine, step, bands) for step in range(1, 4)]
    stacked = jnp.stack(line)

    def pick(h):
        return lax.dynamic_index_in_dim(stacked, (z - h) % 4, axis=0, keepdims=False)

    plane = []
    for flip in range(1, 4):
        payload = jnp.concatenate([pick(c), pick(c ^ NEXT[flip])])
        plane.append(across(payload, flip))
    here = line + plane
    there = [sibling(piece, bands) for piece in here]
    pattern = all_columns(columns, bands, z, c, core)
    tables = address_tables(pattern, z, c, slots_here, 2 * per_piece)
    tables = [table.reshape(-1).astype(jnp.int32) for table in tables]
    origin = jnp.concatenate([jnp.stack([band * rows_here, c, core]).astype(jnp.int32), tables.pop()])
    parts = [(piece, part) for part in (False, True) for piece in (0, 1, 2, 3, 4, 6, 8)]
    count = 17 * 2 * per_piece + 1
    return pl.pallas_call(
        functools.partial(local_iteration, parts, rows, kept, rows_here, slots_here),
        out_shape=jax.ShapeDtypeStruct(values.shape, jnp.float32),
        in_specs=[pl.BlockSpec(memory_space=pltpu.SMEM)] * 5
        + [pl.BlockSpec(memory_space=pl.ANY)] * len(parts),
        out_specs=pl.BlockSpec(memory_space=pltpu.VMEM),
        scratch_shapes=[
            pltpu.VMEM((count, size, size), jnp.bfloat16),
            pltpu.VMEM((rows * kept + 1, size, size), jnp.bfloat16),
            pltpu.VMEM((rows * slots_here + 1, size, size), jnp.bfloat16),
            pltpu.SemaphoreType.DMA((20,)),
        ],
        compiler_params=pltpu.CompilerParams(vmem_limit_bytes=32 * 1024 * 1024),
    )(*tables, origin, *here, *there)


def per_device(values, columns):
    bands, panels = lax.axis_size("row"), lax.axis_size("col")
    if panels == 4 and bands == 8 and values.shape[0] == 2:
        return per_device_whole(values, columns)
    return per_device_panels(values, columns)


def solution(mesh):
    in_specs = (P("row", "col", None, None), P("row", "col"))
    out_specs = P("row", "col", None, None)
    return jax.shard_map(
        per_device, mesh=mesh, in_specs=in_specs, out_specs=out_specs, check_vma=False
    )
```

```python
import jax
import jax.numpy as jnp
from jax import lax
from jax.experimental import pallas as pl
from jax.experimental.pallas import tpu as pltpu
from jax.sharding import PartitionSpec as P

def select_blocks(panel_blocks, panel_slots, row_columns, targets):
    partner = jnp.take(panel_slots, row_columns, axis=0)
    width = partner.shape[2]
    match = partner[:, :, :, None] == targets[:, None, None, :]
    found = jnp.any(match, axis=2)
    where_slot = jnp.sum(
        jnp.where(match, jnp.arange(width, dtype=jnp.int32)[None, None, :, None], 0), axis=2
    )
    picked = panel_blocks[row_columns[:, :, None], where_slot]
    return jnp.where(found[:, :, :, None, None], picked, jnp.zeros((), picked.dtype))


def partial_product(row_blocks, row_columns, panel_blocks, panel_slots, targets):
    picked = select_blocks(panel_blocks, panel_slots, row_columns, targets)
    return jnp.einsum("bsxz,bstzy->btxy", row_blocks, picked, preferred_element_type=jnp.float32)


def gather_panel(blocks):
    return lax.all_gather(blocks, "row", axis=0, tiled=True)


def per_device_panels(values, columns):
    rows_here, slots_here, block = (values.shape[0], values.shape[1], values.shape[2])
    row_ids = lax.axis_index("row") * rows_here + jnp.arange(rows_here, dtype=jnp.int32)
    on_diagonal = (columns == row_ids[:, None]).astype(jnp.float32)
    identity = on_diagonal[:, :, None, None] * jnp.eye(block, dtype=jnp.float32)[None, None, :, :]
    panel_blocks = lax.all_gather(values, "row", axis=0, tiled=True)
    panel_slots = lax.all_gather(columns, "row", axis=0, tiled=True)
    row_blocks = lax.all_gather(values, "col", axis=1, tiled=True)
    row_columns = lax.all_gather(columns, "col", axis=1, tiled=True)
    square = partial_product(row_blocks, row_columns, panel_blocks, panel_slots, columns)
    square_low = square.astype(jnp.bfloat16)
    square_panel = gather_panel(square_low)
    square_rows = lax.all_gather(square_low, "col", axis=1, tiled=True)
    fourth = partial_product(square_rows, row_columns, square_panel, panel_slots, columns)
    polynomial = (15.0 * identity - 10.0 * square_low.astype(jnp.float32) + 3.0 * fourth).astype(
        jnp.bfloat16
    )
    polynomial_panel = gather_panel(polynomial)
    updated = (
        partial_product(row_blocks, row_columns, polynomial_panel, panel_slots, columns) * 0.125
    )
    return updated


NEXT = (0, 2, 3, 1)
TILE = 16


def around(array, step, bands):
    return lax.ppermute(array, "row", [(r, (r + 2 * step) % bands) for r in range(bands)])


def across(array, flip):
    return lax.ppermute(array, "col", [(c, c ^ flip) for c in range(4)])


def sibling(array, bands):
    return lax.ppermute(array, "row", [(r, r ^ 1) for r in range(bands)])


def next_flip(flip):
    return jnp.where(flip == 3, 1, flip + 1)


def local_iteration(
    origin, line, line_there, *rest
):
    here, there = rest[:3], rest[3:6]
    out, xs, ys, qs, numbers, pattern, table, near, used, sem = rest[6:]
    rows, kept, slots, size = 16, 8, 2, 128
    band, c = origin[0], origin[1]
    z, core = lax.div(band, 2), lax.rem(band, 2)
    chunk = 4 * size + TILE

    pieces = []
    for source, side in ((line, core), (line_there, 1 - core)):
        for step in range(4):
            pieces.append((source, step * chunk, step * 8 + side * 4))
    for group, side in ((here, core), (there, 1 - core)):
        for flip in range(3):
            for part in range(2):
                pieces.append(
                    (group[flip], part * chunk, (4 + flip * 2 + part) * 8 + side * 4)
                )

    total = jnp.zeros((TILE, size), jnp.float32)
    for source, first, _ in pieces:
        total += source[first + 4 * size : first + chunk, :].astype(jnp.float32)
    numbers[...] = total[0:8].astype(jnp.int32)
    copy = pltpu.make_async_copy(numbers, pattern, sem)
    copy.start()

    nothing = jnp.zeros((size, size), jnp.bfloat16)
    empty = 17 * 8
    xs[empty] = nothing
    ys[rows * kept] = nothing
    qs[rows * slots] = nothing
    blank = empty + rows * kept * 256

    def clear(at, carry):
        table[at] = blank
        return carry

    lax.fori_loop(0, rows * rows, clear, 0, unroll=16)

    for source, first, place in pieces:
        for b in range(4):
            xs[place + b] = source[first + b * size : first + (b + 1) * size, :]
    for number, piece in enumerate((0, 1, 2, 3, 5, 7, 9)):
        for b in range(8):
            xs[80 + number * 8 + b] = xs[piece * 8 + b].T
    copy.wait()

    def enter(i, j, place, slot):
        table[i * rows + j] = place + (i * kept + slot) * 256
        near[i * kept + slot] = j

    def known(h, g, base, mirror):
        if mirror is not None:
            for local in range(4):
                used[local] = 0
        for il in range(4):
            for t in range(slots):
                i = 4 * h + il
                j = pattern[0, ((h * 2 + il // 2) * 4 + g) * 4 + (il % 2) * slots + t]
                enter(i, j, base + il * slots + t, g * slots + t)
                if mirror is not None:
                    local = j - 4 * g
                    taken = used[local]
                    used[local] = taken + 1
                    enter(j, i, mirror + il * slots + t, h * slots + taken)

    for h in range(4):
        flip = h ^ c
        own = lax.rem(z - h + 4, 4) * 8
        base = jnp.where(flip == 0, own, (4 + (flip - 1) * 2) * 8)
        known(h, h, base, None)
    for first in range(4):
        for second in range(first + 1, 4):
            flip_first, flip_second = first ^ c, second ^ c
            straight = (flip_second == 0) | (
                (flip_first != 0) & (next_flip(flip_second) == (first ^ second))
            )
            h = jnp.where(straight, first, second)
            g = first + second - h
            flip = g ^ c
            own = lax.rem(z - h + 4, 4) * 8
            base = jnp.where(flip == 0, own, (5 + (flip - 1) * 2) * 8)
            mirror = 80 + jnp.where(flip == 0, own, (4 + flip - 1) * 8)
            known(h, g, base, mirror)

    def wide(parts):
        return jnp.concatenate(parts, axis=1)

    def tall(parts):
        return jnp.concatenate(parts, axis=0)

    def dot(left, right):
        return jnp.dot(left, right, preferred_element_type=jnp.float32)

    def x_at(k, j):
        return table[k * rows + j] & 255

    def y_at(k, j):
        return lax.shift_right_logical(table[k * rows + j], 8)

    for home in range(4):

        def square(i, carry):
            ks = [near[i * kept + s] for s in range(kept)]
            left = wide([xs[x_at(i, k)] for k in ks])
            for p in range(home, 4):
                js = ks[p * slots : (p + 1) * slots]
                right = tall([wide([xs[x_at(k, j)] for j in js]) for k in ks])
                product = dot(left, right).astype(jnp.bfloat16)
                for t in range(slots):
                    block = product[:, t * size : (t + 1) * size]
                    ys[i * kept + p * slots + t] = block
                    if p > home:
                        ys[y_at(js[t], i)] = block.T
            return carry

        lax.fori_loop(home * 4, home * 4 + 4, square, 0)

    eye = (
        lax.broadcasted_iota(jnp.int32, (size, size), 0)
        == lax.broadcasted_iota(jnp.int32, (size, size), 1)
    ).astype(jnp.float32)

    def polynomial(i, carry):
        ks = [near[i * kept + s] for s in range(kept)]
        js = [near[i * kept + c * slots + t] for t in range(slots)]
        left = wide([ys[i * kept + s] for s in range(kept)])
        right = tall([wide([ys[y_at(k, j)] for j in js]) for k in ks])
        fourth = dot(left, right)
        for t in range(slots):
            scale = jnp.where(js[t] == i, 15.0, 0.0)
            low = ys[i * kept + c * slots + t].astype(jnp.float32)
            value = scale * eye - 10.0 * low + 3.0 * fourth[:, t * size : (t + 1) * size]
            qs[i * slots + t] = value.astype(jnp.bfloat16)
        return carry

    lax.fori_loop(0, rows, polynomial, 0)

    for a in range(2):
        i = band * 2 + a
        ks = [near[i * kept + s] for s in range(kept)]
        js = [near[i * kept + c * slots + t] for t in range(slots)]

        def q_at(k, j):
            at = y_at(k, j)
            return lax.shift_right_logical(at, 3) * slots + (at & 1)

        left = wide([xs[x_at(i, k)] for k in ks])
        right = tall([wide([qs[q_at(k, j)] for j in js]) for k in ks])
        updated = dot(left, right) * 0.125
        for t in range(slots):
            out[a, t] = updated[:, t * size : (t + 1) * size]


def per_device_whole(values, columns):
    bands = lax.axis_size("row")
    size = values.shape[2]
    band, c = lax.axis_index("row"), lax.axis_index("col")
    z = band // 2
    lane = lax.broadcasted_iota(jnp.int32, (TILE, size), 1)
    line_number = lax.broadcasted_iota(jnp.int32, (TILE, size), 0)
    first = (band * 4 + c) * 4
    tile = jnp.zeros((TILE, size), jnp.int32)
    for m in range(4):
        here = (lane == first + m) & (line_number == 0)
        tile = jnp.where(here, columns[m // 2, m % 2], tile)
    mine = jnp.concatenate([values.reshape(4 * size, size), tile.astype(jnp.bfloat16)])
    line = jnp.concatenate([mine] + [around(mine, step, bands) for step in range(1, 4)])
    stacked = line.reshape(4, *mine.shape)

    def pick(h):
        return lax.dynamic_index_in_dim(stacked, (z - h) % 4, axis=0, keepdims=False)

    here = []
    for flip in range(1, 4):
        payload = jnp.concatenate([pick(c), pick(c ^ NEXT[flip])])
        here.append(across(payload, flip))
    line_there = sibling(line, bands)
    there = [sibling(piece, bands) for piece in here]
    origin = jnp.stack([band, c]).astype(jnp.int32)
    return pl.pallas_call(
        local_iteration,
        out_shape=jax.ShapeDtypeStruct(values.shape, jnp.float32),
        in_specs=[pl.BlockSpec(memory_space=pltpu.SMEM)]
        + [pl.BlockSpec(memory_space=pltpu.VMEM)] * 8,
        out_specs=pl.BlockSpec(memory_space=pltpu.VMEM),
        scratch_shapes=[
            pltpu.VMEM((17 * 8 + 1, size, size), jnp.bfloat16),
            pltpu.VMEM((129, size, size), jnp.bfloat16),
            pltpu.VMEM((33, size, size), jnp.bfloat16),
            pltpu.VMEM((8, size), jnp.int32),
            pltpu.SMEM((8, size), jnp.int32),
            pltpu.SMEM((256,), jnp.int32),
            pltpu.SMEM((128,), jnp.int32),
            pltpu.SMEM((4,), jnp.int32),
            pltpu.SemaphoreType.DMA,
        ],
        compiler_params=pltpu.CompilerParams(vmem_limit_bytes=32 * 1024 * 1024),
    )(origin, line, line_there, *here, *there)


def per_device(values, columns):
    sizes = (lax.axis_size("row"), lax.axis_size("col"), *values.shape)
    if sizes == (8, 4, 2, 2, 128, 128):
        return per_device_whole(values, columns)
    return per_device_panels(values, columns)


def solution(mesh):
    in_specs = (P("row", "col", None, None), P("row", "col"))
    out_specs = P("row", "col", None, None)
    return jax.shard_map(
        per_device, mesh=mesh, in_specs=in_specs, out_specs=out_specs, check_vma=False
    )
```

```python
import jax
import jax.numpy as jnp
from jax import lax
from jax.experimental import pallas as pl
from jax.experimental.pallas import tpu as pltpu
from jax.sharding import PartitionSpec as P

def select_blocks(panel_blocks, panel_slots, row_columns, targets):
    partner = jnp.take(panel_slots, row_columns, axis=0)
    width = partner.shape[2]
    match = partner[:, :, :, None] == targets[:, None, None, :]
    found = jnp.any(match, axis=2)
    where_slot = jnp.sum(
        jnp.where(match, jnp.arange(width, dtype=jnp.int32)[None, None, :, None], 0), axis=2
    )
    picked = panel_blocks[row_columns[:, :, None], where_slot]
    return jnp.where(found[:, :, :, None, None], picked, jnp.zeros((), picked.dtype))


def partial_product(row_blocks, row_columns, panel_blocks, panel_slots, targets):
    picked = select_blocks(panel_blocks, panel_slots, row_columns, targets)
    return jnp.einsum("bsxz,bstzy->btxy", row_blocks, picked, preferred_element_type=jnp.float32)


def gather_panel(blocks):
    return lax.all_gather(blocks, "row", axis=0, tiled=True)


def per_device_panels(values, columns):
    rows_here, slots_here, block = (values.shape[0], values.shape[1], values.shape[2])
    row_ids = lax.axis_index("row") * rows_here + jnp.arange(rows_here, dtype=jnp.int32)
    on_diagonal = (columns == row_ids[:, None]).astype(jnp.float32)
    identity = on_diagonal[:, :, None, None] * jnp.eye(block, dtype=jnp.float32)[None, None, :, :]
    panel_blocks = lax.all_gather(values, "row", axis=0, tiled=True)
    panel_slots = lax.all_gather(columns, "row", axis=0, tiled=True)
    row_blocks = lax.all_gather(values, "col", axis=1, tiled=True)
    row_columns = lax.all_gather(columns, "col", axis=1, tiled=True)
    square = partial_product(row_blocks, row_columns, panel_blocks, panel_slots, columns)
    square_low = square.astype(jnp.bfloat16)
    square_panel = gather_panel(square_low)
    square_rows = lax.all_gather(square_low, "col", axis=1, tiled=True)
    fourth = partial_product(square_rows, row_columns, square_panel, panel_slots, columns)
    polynomial = (15.0 * identity - 10.0 * square_low.astype(jnp.float32) + 3.0 * fourth).astype(
        jnp.bfloat16
    )
    polynomial_panel = gather_panel(polynomial)
    updated = (
        partial_product(row_blocks, row_columns, polynomial_panel, panel_slots, columns) * 0.125
    )
    return updated


NEXT = (0, 2, 3, 1)
TILE = 16


def around(array, step, bands):
    return lax.ppermute(array, "row", [(r, (r + 2 * step) % bands) for r in range(bands)])


def across(array, flip):
    return lax.ppermute(array, "col", [(c, c ^ flip) for c in range(4)])


def sibling(array, bands):
    return lax.ppermute(array, "row", [(r, r ^ 1) for r in range(bands)])


def next_flip(flip):
    return jnp.where(flip == 3, 1, flip + 1)


def local_iteration(origin, *rest):
    lines, planes = rest[:4], rest[4:16]
    out, xs, ys, qs, numbers, pattern, x_table, y_table, near, sem = rest[16:]
    rows, kept, slots, size = 16, 8, 2, 128
    band, c = origin[0], origin[1]
    z, core = lax.div(band, 2), lax.rem(band, 2)
    half = slots * size

    pieces = []
    total = jnp.zeros((TILE, size), jnp.float32)
    for a in range(2):
        long = half + a * TILE
        for source, side in ((lines[a], core), (lines[2 + a], 1 - core)):
            for step in range(4):
                pieces.append((source, step * long, step * 8 + side * 4 + a * 2))
                if a == 1:
                    total += source[step * long + half : step * long + long, :].astype(jnp.float32)
        for group, side in ((planes[a * 3 : a * 3 + 3], core), (planes[6 + a * 3 : 9 + a * 3], 1 - core)):
            for flip in range(3):
                for part in range(2):
                    place = (4 + flip * 2 + part) * 8 + side * 4 + a * 2
                    pieces.append((group[flip], part * half, place))
                if a == 1:
                    total += group[flip][2 * half : 2 * half + TILE, :].astype(jnp.float32)
    numbers[...] = total[0:8].astype(jnp.int32)
    copy = pltpu.make_async_copy(numbers, pattern, sem)
    copy.start()

    nothing = jnp.zeros((size, size), jnp.bfloat16)
    empty = 17 * 8
    xs[empty] = nothing
    ys[rows * kept] = nothing
    qs[rows * slots] = nothing

    def clear(at, carry):
        x_table[at] = empty
        y_table[at] = rows * kept
        return carry

    lax.fori_loop(0, rows * rows, clear, 0, unroll=16)

    for source, first, place in pieces:
        for b in range(slots):
            xs[place + b] = source[first + b * size : first + (b + 1) * size, :]
    for number, piece in enumerate((0, 1, 2, 3, 5, 7, 9)):
        for b in range(8):
            xs[80 + number * 8 + b] = xs[piece * 8 + b].T
    copy.wait()

    def entries(h, g):
        for il in range(4):
            for t in range(slots):
                j = pattern[0, ((h * 2 + il // 2) * 4 + g) * 4 + (il % 2) * slots + t]
                yield 4 * h + il, j, il * slots + t, g * slots + t

    for h in range(4):
        for g in range(4):
            flip = g ^ c
            own = lax.rem(z - h + 4, 4) * 8
            if h == g:
                base = jnp.where(flip == 0, own, (4 + (flip - 1) * 2) * 8)
            else:
                straight = (flip == 0) | (((h ^ c) != 0) & (next_flip(flip) == (h ^ g)))
                base = jnp.where(flip == 0, own, (5 + (flip - 1) * 2) * 8)
                mirror = 80 + jnp.where(flip == 0, own, (3 + flip) * 8)
            for i, j, number, slot in entries(h, g):
                near[i * kept + slot] = j
                y_table[i * rows + j] = i * kept + slot
                if h == g:
                    x_table[i * rows + j] = base + number
            if h != g:

                @pl.when(straight)
                def _():
                    for i, j, number, slot in entries(h, g):
                        x_table[i * rows + j] = base + number
                        x_table[j * rows + i] = mirror + number

    def wide(parts):
        return jnp.concatenate(parts, axis=1)

    def tall(parts):
        return jnp.concatenate(parts, axis=0)

    def dot(left, right):
        return jnp.dot(left, right, preferred_element_type=jnp.float32)

    def x_at(k, j):
        return x_table[k * rows + j]

    def y_at(k, j):
        return y_table[k * rows + j]

    for home in range(4):

        def square(i, carry):
            ks = [near[i * kept + s] for s in range(kept)]
            left = wide([xs[x_at(i, k)] for k in ks])
            js = ks[home * slots :]
            right = tall([wide([xs[x_at(k, j)] for j in js]) for k in ks])
            product = dot(left, right).astype(jnp.bfloat16)
            for t, j in enumerate(js):
                block = product[:, t * size : (t + 1) * size]
                ys[i * kept + home * slots + t] = block
                if t >= slots:
                    ys[y_at(j, i)] = block.T
            return carry

        lax.fori_loop(home * 4, home * 4 + 4, square, 0)

    eye = (
        lax.broadcasted_iota(jnp.int32, (size, size), 0)
        == lax.broadcasted_iota(jnp.int32, (size, size), 1)
    ).astype(jnp.float32)

    def polynomial(i, carry):
        ks = [near[i * kept + s] for s in range(kept)]
        js = [near[i * kept + c * slots + t] for t in range(slots)]
        left = wide([ys[i * kept + s] for s in range(kept)])
        right = tall([wide([ys[y_at(k, j)] for j in js]) for k in ks])
        fourth = dot(left, right)
        for t in range(slots):
            scale = jnp.where(js[t] == i, 15.0, 0.0)
            low = ys[i * kept + c * slots + t].astype(jnp.float32)
            value = scale * eye - 10.0 * low + 3.0 * fourth[:, t * size : (t + 1) * size]
            qs[i * slots + t] = value.astype(jnp.bfloat16)
        return carry

    lax.fori_loop(0, rows, polynomial, 0)

    for a in range(2):
        i = band * 2 + a
        ks = [near[i * kept + s] for s in range(kept)]
        js = [near[i * kept + c * slots + t] for t in range(slots)]

        def q_at(k, j):
            at = y_at(k, j)
            return lax.shift_right_logical(at, 3) * slots + (at & 1)

        left = wide([xs[x_at(i, k)] for k in ks])
        right = tall([wide([qs[q_at(k, j)] for j in js]) for k in ks])
        updated = dot(left, right) * 0.125
        for t in range(slots):
            out[a, t] = updated[:, t * size : (t + 1) * size]


def per_device_whole(values, columns):
    bands = lax.axis_size("row")
    size = values.shape[2]
    band, c = lax.axis_index("row"), lax.axis_index("col")
    z = band // 2
    lane = lax.broadcasted_iota(jnp.int32, (TILE, size), 1)
    line_number = lax.broadcasted_iota(jnp.int32, (TILE, size), 0)
    first = (band * 4 + c) * 4
    tile = jnp.zeros((TILE, size), jnp.int32)
    for m in range(4):
        here = (lane == first + m) & (line_number == 0)
        tile = jnp.where(here, columns[m // 2, m % 2], tile)
    halves = values.reshape(2, 2 * size, size)
    mine = (halves[0], jnp.concatenate([halves[1], tile.astype(jnp.bfloat16)]))

    def from_line(line, h):
        return lax.dynamic_index_in_dim(line, (z - h) % 4, axis=0, keepdims=False)

    lines = [
        jnp.stack([half] + [around(half, step, bands) for step in range(1, 4)]) for half in mine
    ]
    here, lines_there = [], []
    for a, line in enumerate(lines):
        tail = [jnp.sum(line[:, 2 * size :], axis=0)] if a else []
        for flip in range(1, 4):
            parts = [from_line(line, h)[: 2 * size] for h in (c, c ^ NEXT[flip])]
            here.append(across(jnp.concatenate(parts + tail), flip))
        lines_there.append(sibling(line.reshape(-1, size), bands))
    there = [sibling(piece, bands) for piece in here]
    lines = [line.reshape(-1, size) for line in lines]
    origin = jnp.stack([band, c]).astype(jnp.int32)
    return pl.pallas_call(
        local_iteration,
        out_shape=jax.ShapeDtypeStruct(values.shape, jnp.float32),
        in_specs=[pl.BlockSpec(memory_space=pltpu.SMEM)]
        + [pl.BlockSpec(memory_space=pltpu.VMEM)] * 16,
        out_specs=pl.BlockSpec(memory_space=pltpu.VMEM),
        scratch_shapes=[
            pltpu.VMEM((17 * 8 + 1, size, size), jnp.bfloat16),
            pltpu.VMEM((129, size, size), jnp.bfloat16),
            pltpu.VMEM((33, size, size), jnp.bfloat16),
            pltpu.VMEM((8, size), jnp.int32),
            pltpu.SMEM((8, size), jnp.int32),
            pltpu.SMEM((256,), jnp.int32),
            pltpu.SMEM((256,), jnp.int32),
            pltpu.SMEM((128,), jnp.int32),
            pltpu.SemaphoreType.DMA,
        ],
        compiler_params=pltpu.CompilerParams(vmem_limit_bytes=32 * 1024 * 1024),
    )(origin, *lines, *lines_there, *here, *there)


def per_device(values, columns):
    sizes = (lax.axis_size("row"), lax.axis_size("col"), *values.shape)
    if sizes == (8, 4, 2, 2, 128, 128):
        return per_device_whole(values, columns)
    return per_device_panels(values, columns)


def solution(mesh):
    in_specs = (P("row", "col", None, None), P("row", "col"))
    out_specs = P("row", "col", None, None)
    return jax.shard_map(
        per_device, mesh=mesh, in_specs=in_specs, out_specs=out_specs, check_vma=False
    )
```

```python
import jax
import jax.numpy as jnp
from jax import lax
from jax.experimental import pallas as pl
from jax.experimental.pallas import tpu as pltpu
from jax.sharding import PartitionSpec as P

def select_blocks(panel_blocks, panel_slots, row_columns, targets):
    partner = jnp.take(panel_slots, row_columns, axis=0)
    width = partner.shape[2]
    match = partner[:, :, :, None] == targets[:, None, None, :]
    found = jnp.any(match, axis=2)
    where_slot = jnp.sum(
        jnp.where(match, jnp.arange(width, dtype=jnp.int32)[None, None, :, None], 0), axis=2
    )
    picked = panel_blocks[row_columns[:, :, None], where_slot]
    return jnp.where(found[:, :, :, None, None], picked, jnp.zeros((), picked.dtype))


def partial_product(row_blocks, row_columns, panel_blocks, panel_slots, targets):
    picked = select_blocks(panel_blocks, panel_slots, row_columns, targets)
    return jnp.einsum("bsxz,bstzy->btxy", row_blocks, picked, preferred_element_type=jnp.float32)


def gather_panel(blocks):
    return lax.all_gather(blocks, "row", axis=0, tiled=True)


def per_device_panels(values, columns):
    rows_here, slots_here, block = (values.shape[0], values.shape[1], values.shape[2])
    row_ids = lax.axis_index("row") * rows_here + jnp.arange(rows_here, dtype=jnp.int32)
    on_diagonal = (columns == row_ids[:, None]).astype(jnp.float32)
    identity = on_diagonal[:, :, None, None] * jnp.eye(block, dtype=jnp.float32)[None, None, :, :]
    panel_blocks = lax.all_gather(values, "row", axis=0, tiled=True)
    panel_slots = lax.all_gather(columns, "row", axis=0, tiled=True)
    row_blocks = lax.all_gather(values, "col", axis=1, tiled=True)
    row_columns = lax.all_gather(columns, "col", axis=1, tiled=True)
    square = partial_product(row_blocks, row_columns, panel_blocks, panel_slots, columns)
    square_low = square.astype(jnp.bfloat16)
    square_panel = gather_panel(square_low)
    square_rows = lax.all_gather(square_low, "col", axis=1, tiled=True)
    fourth = partial_product(square_rows, row_columns, square_panel, panel_slots, columns)
    polynomial = (15.0 * identity - 10.0 * square_low.astype(jnp.float32) + 3.0 * fourth).astype(
        jnp.bfloat16
    )
    polynomial_panel = gather_panel(polynomial)
    updated = (
        partial_product(row_blocks, row_columns, polynomial_panel, panel_slots, columns) * 0.125
    )
    return updated


TILE = 16


def around(array, step, bands):
    return lax.ppermute(array, "row", [(r, (r + 2 * step) % bands) for r in range(bands)])


def exchange(array):
    return lax.all_to_all(array, "col", 0, 0, tiled=False)


def sibling(array, bands):
    return lax.ppermute(array, "row", [(r, r ^ 1) for r in range(bands)])


def next_flip(flip):
    return jnp.where(flip == 3, 1, jnp.where(flip == 0, 0, flip + 1))


def make_payloads(place, columns, values, first, second):
    size = values.shape[2]
    lane = lax.broadcasted_iota(jnp.int32, (TILE, size), 1)
    line = lax.broadcasted_iota(jnp.int32, (TILE, size), 0)
    tile = jnp.zeros((TILE, size), jnp.int32)
    for m in range(4):
        here = (lane == place[0] + m) & (line == 0)
        tile = jnp.where(here, columns[m // 2, m % 2], tile)
    for t in range(2):
        first[t * size : (t + 1) * size, :] = values[0, t]
        second[t * size : (t + 1) * size, :] = values[1, t]
    first[2 * size :, :] = tile.astype(jnp.float32).astype(jnp.bfloat16)


def local_iteration(origin, *rest):
    lines, planes = rest[:4], rest[4:8]
    out, xs, ys, qs, numbers, pattern, x_table, y_table, near, sem = rest[8:]
    rows, kept, slots, size = 16, 8, 2, 128
    band, c = origin[0], origin[1]
    z, core = lax.div(band, 2), lax.rem(band, 2)
    half = slots * size

    pieces = []
    total = jnp.zeros((TILE, size), jnp.float32)

    def add_tile(source, first):
        rows_at = pl.ds(pl.multiple_of(first, TILE), TILE)
        return total + source[rows_at, :].astype(jnp.float32)

    for a in range(2):
        tail = 0 if a else TILE
        for group, side in ((0, core), (2, 1 - core)):
            source = lines[group + a]
            for step in range(4):
                first = step * (half + tail)
                pieces.append((source, first, step * 8 + side * 4 + a * 2))
                if tail:
                    total = add_tile(source, first + half)
            source = planes[group + a]
            for flip in range(1, 4):
                first = (c ^ flip) * (2 * half + tail)
                for part in range(2):
                    place = (2 + flip * 2 + part) * 8 + side * 4 + a * 2
                    pieces.append((source, first + part * half, place))
                if tail:
                    total = add_tile(source, first + 2 * half)
    numbers[...] = total[0:8].astype(jnp.int32)
    copy = pltpu.make_async_copy(numbers, pattern, sem)
    copy.start()

    nothing = jnp.zeros((size, size), jnp.bfloat16)
    empty = 17 * 8
    xs[empty] = nothing
    ys[rows * kept] = nothing
    qs[rows * slots] = nothing

    def clear(at, carry):
        x_table[at] = empty
        y_table[at] = rows * kept
        return carry

    lax.fori_loop(0, rows * rows, clear, 0, unroll=16)

    for source, first, place in pieces:
        for b in range(slots):
            xs[place + b] = source[pl.ds(pl.multiple_of(first + b * size, TILE), size), :]
    for number, piece in enumerate((0, 1, 2, 3, 5, 7, 9)):
        for b in range(8):
            xs[80 + number * 8 + b] = xs[piece * 8 + b].T
    copy.wait()

    def entries(h, g):
        for il in range(4):
            for t in range(slots):
                j = pattern[0, ((h * 2 + il // 2) * 4 + g) * 4 + (il % 2) * slots + t]
                yield 4 * h + il, j, il * slots + t, g * slots + t

    for h in range(4):
        for g in range(4):
            flip = g ^ c
            own = lax.rem(z - h + 4, 4) * 8
            if h == g:
                base = jnp.where(flip == 0, own, (4 + (flip - 1) * 2) * 8)
            else:
                straight = (flip == 0) | (((h ^ c) != 0) & (next_flip(flip) == (h ^ g)))
                base = jnp.where(flip == 0, own, (5 + (flip - 1) * 2) * 8)
                mirror = 80 + jnp.where(flip == 0, own, (3 + flip) * 8)
            for i, j, number, slot in entries(h, g):
                near[i * kept + slot] = j
                y_table[i * rows + j] = i * kept + slot
                if h == g:
                    x_table[i * rows + j] = base + number
            if h != g:

                @pl.when(straight)
                def _():
                    for i, j, number, slot in entries(h, g):
                        x_table[i * rows + j] = base + number
                        x_table[j * rows + i] = mirror + number

    def wide(parts):
        return jnp.concatenate(parts, axis=1)

    def tall(parts):
        return jnp.concatenate(parts, axis=0)

    def dot(left, right):
        return jnp.dot(left, right, preferred_element_type=jnp.float32)

    def x_at(k, j):
        return x_table[k * rows + j]

    def y_at(k, j):
        return y_table[k * rows + j]

    for home in range(4):

        def square(i, carry):
            ks = [near[i * kept + s] for s in range(kept)]
            left = wide([xs[x_at(i, k)] for k in ks])
            js = ks[home * slots :]
            right = tall([wide([xs[x_at(k, j)] for j in js]) for k in ks])
            product = dot(left, right).astype(jnp.bfloat16)
            for t, j in enumerate(js):
                block = product[:, t * size : (t + 1) * size]
                ys[i * kept + home * slots + t] = block
                if t >= slots:
                    ys[y_at(j, i)] = block.T
            return carry

        lax.fori_loop(home * 4, home * 4 + 4, square, 0)

    eye = (
        lax.broadcasted_iota(jnp.int32, (size, size), 0)
        == lax.broadcasted_iota(jnp.int32, (size, size), 1)
    ).astype(jnp.float32)

    def polynomial(i, carry):
        ks = [near[i * kept + s] for s in range(kept)]
        js = [near[i * kept + c * slots + t] for t in range(slots)]
        left = wide([ys[i * kept + s] for s in range(kept)])
        right = tall([wide([ys[y_at(k, j)] for j in js]) for k in ks])
        fourth = dot(left, right)
        for t in range(slots):
            scale = jnp.where(js[t] == i, 15.0, 0.0)
            low = ys[i * kept + c * slots + t].astype(jnp.float32)
            value = scale * eye - 10.0 * low + 3.0 * fourth[:, t * size : (t + 1) * size]
            qs[i * slots + t] = value.astype(jnp.bfloat16)
        return carry

    lax.fori_loop(0, rows, polynomial, 0)

    for a in range(2):
        i = band * 2 + a
        ks = [near[i * kept + s] for s in range(kept)]
        js = [near[i * kept + c * slots + t] for t in range(slots)]

        def q_at(k, j):
            at = y_at(k, j)
            return lax.shift_right_logical(at, 3) * slots + (at & 1)

        left = wide([xs[x_at(i, k)] for k in ks])
        right = tall([wide([qs[q_at(k, j)] for j in js]) for k in ks])
        updated = dot(left, right) * 0.125
        for t in range(slots):
            out[a, t] = updated[:, t * size : (t + 1) * size]


def per_device_whole(values, columns):
    bands = lax.axis_size("row")
    size = values.shape[2]
    band, c = lax.axis_index("row"), lax.axis_index("col")
    z = band // 2
    origin = jnp.stack([band, c]).astype(jnp.int32)
    place = ((band * 4 + c) * 4).reshape(1).astype(jnp.int32)
    mine = pl.pallas_call(
        make_payloads,
        out_shape=[
            jax.ShapeDtypeStruct((2 * size + TILE, size), jnp.bfloat16),
            jax.ShapeDtypeStruct((2 * size, size), jnp.bfloat16),
        ],
        in_specs=[
            pl.BlockSpec(memory_space=pltpu.SMEM),
            pl.BlockSpec(memory_space=pltpu.SMEM),
            pl.BlockSpec(memory_space=pltpu.VMEM),
        ],
        out_specs=[pl.BlockSpec(memory_space=pltpu.VMEM)] * 2,
    )(place, columns, values)

    def from_line(line, h):
        return lax.dynamic_index_in_dim(line, (z - h) % 4, axis=0, keepdims=False)

    lines = [
        jnp.stack([half] + [around(half, step, bands) for step in range(1, 4)]) for half in mine
    ]
    here = []
    for a, line in enumerate(lines):
        tail = [] if a else [jnp.sum(line[:, 2 * size :], axis=0)]
        parts = []
        for to in range(4):
            picks = [from_line(line, h)[: 2 * size] for h in (c, c ^ next_flip(c ^ to))]
            parts.append(jnp.concatenate(picks + tail))
        here.append(exchange(jnp.stack(parts)).reshape(-1, size))
    lines = [line.reshape(-1, size) for line in lines]
    lines_there = [sibling(line, bands) for line in lines]
    there = [sibling(piece, bands) for piece in here]
    return pl.pallas_call(
        local_iteration,
        out_shape=jax.ShapeDtypeStruct(values.shape, jnp.float32),
        in_specs=[pl.BlockSpec(memory_space=pltpu.SMEM)]
        + [pl.BlockSpec(memory_space=pltpu.VMEM)] * 8,
        out_specs=pl.BlockSpec(memory_space=pltpu.VMEM),
        scratch_shapes=[
            pltpu.VMEM((17 * 8 + 1, size, size), jnp.bfloat16),
            pltpu.VMEM((129, size, size), jnp.bfloat16),
            pltpu.VMEM((33, size, size), jnp.bfloat16),
            pltpu.VMEM((8, size), jnp.int32),
            pltpu.SMEM((8, size), jnp.int32),
            pltpu.SMEM((256,), jnp.int32),
            pltpu.SMEM((256,), jnp.int32),
            pltpu.SMEM((128,), jnp.int32),
            pltpu.SemaphoreType.DMA,
        ],
        compiler_params=pltpu.CompilerParams(vmem_limit_bytes=32 * 1024 * 1024),
    )(origin, *lines, *lines_there, *here, *there)


def per_device(values, columns):
    sizes = (lax.axis_size("row"), lax.axis_size("col"), *values.shape)
    if sizes == (8, 4, 2, 2, 128, 128):
        return per_device_whole(values, columns)
    return per_device_panels(values, columns)


def solution(mesh):
    in_specs = (P("row", "col", None, None), P("row", "col"))
    out_specs = P("row", "col", None, None)
    return jax.shard_map(
        per_device, mesh=mesh, in_specs=in_specs, out_specs=out_specs, check_vma=False
    )
```

```python
import jax
import jax.numpy as jnp
from jax import lax
from jax.experimental import pallas as pl
from jax.experimental.pallas import tpu as pltpu
from jax.sharding import PartitionSpec as P

def select_blocks(panel_blocks, panel_slots, row_columns, targets):
    partner = jnp.take(panel_slots, row_columns, axis=0)
    width = partner.shape[2]
    match = partner[:, :, :, None] == targets[:, None, None, :]
    found = jnp.any(match, axis=2)
    where_slot = jnp.sum(
        jnp.where(match, jnp.arange(width, dtype=jnp.int32)[None, None, :, None], 0), axis=2
    )
    picked = panel_blocks[row_columns[:, :, None], where_slot]
    return jnp.where(found[:, :, :, None, None], picked, jnp.zeros((), picked.dtype))


def partial_product(row_blocks, row_columns, panel_blocks, panel_slots, targets):
    picked = select_blocks(panel_blocks, panel_slots, row_columns, targets)
    return jnp.einsum("bsxz,bstzy->btxy", row_blocks, picked, preferred_element_type=jnp.float32)


def gather_panel(blocks):
    return lax.all_gather(blocks, "row", axis=0, tiled=True)


def per_device_panels(values, columns):
    rows_here, slots_here, block = (values.shape[0], values.shape[1], values.shape[2])
    row_ids = lax.axis_index("row") * rows_here + jnp.arange(rows_here, dtype=jnp.int32)
    on_diagonal = (columns == row_ids[:, None]).astype(jnp.float32)
    identity = on_diagonal[:, :, None, None] * jnp.eye(block, dtype=jnp.float32)[None, None, :, :]
    panel_blocks = lax.all_gather(values, "row", axis=0, tiled=True)
    panel_slots = lax.all_gather(columns, "row", axis=0, tiled=True)
    row_blocks = lax.all_gather(values, "col", axis=1, tiled=True)
    row_columns = lax.all_gather(columns, "col", axis=1, tiled=True)
    square = partial_product(row_blocks, row_columns, panel_blocks, panel_slots, columns)
    square_low = square.astype(jnp.bfloat16)
    square_panel = gather_panel(square_low)
    square_rows = lax.all_gather(square_low, "col", axis=1, tiled=True)
    fourth = partial_product(square_rows, row_columns, square_panel, panel_slots, columns)
    polynomial = (15.0 * identity - 10.0 * square_low.astype(jnp.float32) + 3.0 * fourth).astype(
        jnp.bfloat16
    )
    polynomial_panel = gather_panel(polynomial)
    updated = (
        partial_product(row_blocks, row_columns, polynomial_panel, panel_slots, columns) * 0.125
    )
    return updated


TILE = 16


def around(array, step, bands):
    return lax.ppermute(array, "row", [(r, (r + 2 * step) % bands) for r in range(bands)])


def across(array, flip):
    return lax.ppermute(array, "col", [(c, c ^ flip) for c in range(4)])


def sibling(array, bands):
    return lax.ppermute(array, "row", [(r, r ^ 1) for r in range(bands)])


def next_flip(flip):
    return flip % 3 + 1


def make_payloads(place, columns, values, first, second):
    size = values.shape[2]
    lane = lax.broadcasted_iota(jnp.int32, (TILE, size), 1)
    line = lax.broadcasted_iota(jnp.int32, (TILE, size), 0)
    tile = jnp.zeros((TILE, size), jnp.int32)
    for m in range(4):
        here = (lane == place[0] + m) & (line == 0)
        tile = jnp.where(here, columns[m // 2, m % 2], tile)
    for t in range(2):
        first[t * size : (t + 1) * size, :] = values[0, t]
        second[t * size : (t + 1) * size, :] = values[1, t]
    first[2 * size :, :] = tile.astype(jnp.float32).astype(jnp.bfloat16)


def line_pieces(lines, core, a):
    skip, long = (4 * (256 + TILE), 256) if a else (0, 256 + TILE)
    for source, side in zip(lines, (core, 1 - core)):
        for step in range(4):
            yield source, skip + step * long, step * 8 + side * 4 + a * 2


def plane_pieces(planes, core, a):
    for source, side in zip(planes, (core, 1 - core)):
        for flip in range(3):
            for part in range(2):
                place = (4 + flip * 2 + part) * 8 + side * 4 + a * 2
                if a:
                    yield source[flip], part * 256, place
                else:
                    yield source, flip * (512 + TILE) + part * 256, place


def put(blocks, source, first, place, piece, mirrors):
    size = blocks.shape[1]
    for b in range(2):
        block = source[first + b * size : first + (b + 1) * size, :]
        blocks[place + b] = block
        if piece in mirrors:
            blocks[80 + mirrors.index(piece) * 8 + place - piece * 8 + b] = block.T


MIRRORS = (0, 1, 2, 3, 5, 7, 9)


def fold_first(origin, *rest):
    lines, planes = rest[:2], rest[2:4]
    blocks, x_table, y_table, near, numbers, pattern, sem = rest[4:]
    rows, kept, slots, size = 16, 8, 2, 128
    band, c = origin[0], origin[1]
    z, core = lax.div(band, 2), lax.rem(band, 2)

    total = jnp.zeros((TILE, size), jnp.float32)
    for source, first, _ in line_pieces(lines, core, 0):
        total += source[first + 2 * size : first + 2 * size + TILE, :].astype(jnp.float32)
    for source in planes:
        for flip in range(3):
            end = (flip + 1) * (4 * size + TILE)
            total += source[end - TILE : end, :].astype(jnp.float32)
    numbers[...] = total[0:8].astype(jnp.int32)
    copy = pltpu.make_async_copy(numbers, pattern, sem)
    copy.start()

    empty = 17 * 8
    blocks[empty] = jnp.zeros((size, size), jnp.bfloat16)

    def clear(at, carry):
        x_table[at] = empty
        y_table[at] = rows * kept
        return carry

    lax.fori_loop(0, rows * rows, clear, 0, unroll=16)

    for a in range(2):
        for number, item in enumerate(line_pieces(lines, core, a)):
            put(blocks, *item, number % 4, MIRRORS)
    for number, item in enumerate(plane_pieces(planes, core, 0)):
        put(blocks, *item, 4 + number % 6, MIRRORS)
    copy.wait()

    def entries(h, g):
        for il in range(4):
            for t in range(slots):
                j = pattern[0, ((h * 2 + il // 2) * 4 + g) * 4 + (il % 2) * slots + t]
                yield 4 * h + il, j, il * slots + t, g * slots + t

    for h in range(4):
        for g in range(4):
            flip = g ^ c
            own = lax.rem(z - h + 4, 4) * 8
            if h == g:
                base = jnp.where(flip == 0, own, (4 + (flip - 1) * 2) * 8)
            else:
                straight = (flip == 0) | (((h ^ c) != 0) & (lax.rem(flip, 3) + 1 == (h ^ g)))
                base = jnp.where(flip == 0, own, (5 + (flip - 1) * 2) * 8)
                mirror = 80 + jnp.where(flip == 0, own, (3 + flip) * 8)
            for i, j, number, slot in entries(h, g):
                near[i * kept + slot] = j
                y_table[i * rows + j] = i * kept + slot
                if h == g:
                    x_table[i * rows + j] = base + number
            if h != g:

                @pl.when(straight)
                def _():
                    for i, j, number, slot in entries(h, g):
                        x_table[i * rows + j] = base + number
                        x_table[j * rows + i] = mirror + number


def local_iteration(origin, x_table, y_table, near, blocks, *rest):
    planes, (out, xs, ys, qs) = (rest[:3], rest[3:6]), rest[6:]
    rows, kept, slots, size = 16, 8, 2, 128
    band, c = origin[0], origin[1]
    core = lax.rem(band, 2)
    nothing = jnp.zeros((size, size), jnp.bfloat16)
    ys[rows * kept] = nothing
    qs[rows * slots] = nothing
    for at in range(blocks.shape[0]):
        xs[at] = blocks[at]
    for number, item in enumerate(plane_pieces(planes, core, 1)):
        put(xs, *item, 4 + number % 6, MIRRORS)

    def wide(parts):
        return jnp.concatenate(parts, axis=1)

    def tall(parts):
        return jnp.concatenate(parts, axis=0)

    def dot(left, right):
        return jnp.dot(left, right, preferred_element_type=jnp.float32)

    def x_at(k, j):
        return x_table[k * rows + j]

    def y_at(k, j):
        return y_table[k * rows + j]

    for home in range(4):

        def square(i, carry):
            ks = [near[i * kept + s] for s in range(kept)]
            left = wide([xs[x_at(i, k)] for k in ks])
            js = ks[home * slots :]
            right = tall([wide([xs[x_at(k, j)] for j in js]) for k in ks])
            product = dot(left, right).astype(jnp.bfloat16)
            for t, j in enumerate(js):
                block = product[:, t * size : (t + 1) * size]
                ys[i * kept + home * slots + t] = block
                if t >= slots:
                    ys[y_at(j, i)] = block.T
            return carry

        lax.fori_loop(home * 4, home * 4 + 4, square, 0)

    eye = (
        lax.broadcasted_iota(jnp.int32, (size, size), 0)
        == lax.broadcasted_iota(jnp.int32, (size, size), 1)
    ).astype(jnp.float32)

    def polynomial(i, carry):
        ks = [near[i * kept + s] for s in range(kept)]
        js = [near[i * kept + c * slots + t] for t in range(slots)]
        left = wide([ys[i * kept + s] for s in range(kept)])
        right = tall([wide([ys[y_at(k, j)] for j in js]) for k in ks])
        fourth = dot(left, right)
        for t in range(slots):
            scale = jnp.where(js[t] == i, 15.0, 0.0)
            low = ys[i * kept + c * slots + t].astype(jnp.float32)
            value = scale * eye - 10.0 * low + 3.0 * fourth[:, t * size : (t + 1) * size]
            qs[i * slots + t] = value.astype(jnp.bfloat16)
        return carry

    lax.fori_loop(0, rows, polynomial, 0)

    for a in range(2):
        i = band * 2 + a
        ks = [near[i * kept + s] for s in range(kept)]
        js = [near[i * kept + c * slots + t] for t in range(slots)]

        def q_at(k, j):
            at = y_at(k, j)
            return lax.shift_right_logical(at, 3) * slots + (at & 1)

        left = wide([xs[x_at(i, k)] for k in ks])
        right = tall([wide([qs[q_at(k, j)] for j in js]) for k in ks])
        updated = dot(left, right) * 0.125
        for t in range(slots):
            out[a, t] = updated[:, t * size : (t + 1) * size]


def per_device_whole(values, columns):
    bands = lax.axis_size("row")
    size = values.shape[2]
    band, c = lax.axis_index("row"), lax.axis_index("col")
    z = band // 2
    origin = jnp.stack([band, c]).astype(jnp.int32)
    place = ((band * 4 + c) * 4).reshape(1).astype(jnp.int32)
    mine = pl.pallas_call(
        make_payloads,
        out_shape=[
            jax.ShapeDtypeStruct((2 * size + TILE, size), jnp.bfloat16),
            jax.ShapeDtypeStruct((2 * size, size), jnp.bfloat16),
        ],
        in_specs=[
            pl.BlockSpec(memory_space=pltpu.SMEM),
            pl.BlockSpec(memory_space=pltpu.SMEM),
            pl.BlockSpec(memory_space=pltpu.VMEM),
        ],
        out_specs=[pl.BlockSpec(memory_space=pltpu.VMEM)] * 2,
    )(place, columns, values)

    def from_line(line, h):
        return lax.dynamic_index_in_dim(line, (z - h) % 4, axis=0, keepdims=False)

    def col_payloads(line):
        line = line.reshape(4, -1, size)
        tail = [jnp.sum(line[:, 2 * size :], axis=0)] if line.shape[1] > 2 * size else []
        for flip in range(1, 4):
            parts = [from_line(line, h)[: 2 * size] for h in (c, c ^ next_flip(flip))]
            yield jnp.concatenate(parts + tail)

    line = [around(mine[0], step, bands) for step in range(1, 4)]
    later, line[2] = lax.optimization_barrier((mine[1], line[2]))
    line = jnp.concatenate([mine[0]] + line)
    later_line = [around(later, step, bands) for step in range(1, 4)]
    later_line = jnp.concatenate([later] + later_line)
    first = [across(payload, flip + 1) for flip, payload in enumerate(col_payloads(line))]
    later_line, first[2] = lax.optimization_barrier((later_line, first[2]))
    second = [across(payload, flip + 1) for flip, payload in enumerate(col_payloads(later_line))]
    lines = jnp.concatenate([line, later_line])
    lines_there = sibling(lines, bands)
    first = jnp.concatenate(first)
    first_there = sibling(first, bands)
    smem, vmem = pl.BlockSpec(memory_space=pltpu.SMEM), pl.BlockSpec(memory_space=pltpu.VMEM)
    limit = pltpu.CompilerParams(vmem_limit_bytes=32 * 1024 * 1024)
    count = 17 * 8 + 1
    blocks, *tables = pl.pallas_call(
        fold_first,
        out_shape=[
            jax.ShapeDtypeStruct((count, size, size), jnp.bfloat16),
            jax.ShapeDtypeStruct((256,), jnp.int32),
            jax.ShapeDtypeStruct((256,), jnp.int32),
            jax.ShapeDtypeStruct((128,), jnp.int32),
        ],
        in_specs=[smem] + [vmem] * 4,
        out_specs=[vmem, smem, smem, smem],
        scratch_shapes=[
            pltpu.VMEM((8, size), jnp.int32),
            pltpu.SMEM((8, size), jnp.int32),
            pltpu.SemaphoreType.DMA,
        ],
        compiler_params=limit,
        cost_estimate=pl.CostEstimate(
            flops=100_000_000, bytes_accessed=8_000_000, transcendentals=0
        ),
    )(origin, lines, lines_there, first, first_there)
    blocks, *second = lax.optimization_barrier((blocks, *second))
    second_there = [sibling(piece, bands) for piece in second]
    return pl.pallas_call(
        local_iteration,
        out_shape=jax.ShapeDtypeStruct(values.shape, jnp.float32),
        in_specs=[smem] * 4 + [vmem] * 7,
        out_specs=vmem,
        scratch_shapes=[
            pltpu.VMEM((count, size, size), jnp.bfloat16),
            pltpu.VMEM((129, size, size), jnp.bfloat16),
            pltpu.VMEM((33, size, size), jnp.bfloat16),
        ],
        compiler_params=limit,
    )(origin, *tables, blocks, *second, *second_there)


def per_device(values, columns):
    sizes = (lax.axis_size("row"), lax.axis_size("col"), *values.shape)
    if sizes == (8, 4, 2, 2, 128, 128):
        return per_device_whole(values, columns)
    return per_device_panels(values, columns)


def solution(mesh):
    in_specs = (P("row", "col", None, None), P("row", "col"))
    out_specs = P("row", "col", None, None)
    return jax.shard_map(
        per_device, mesh=mesh, in_specs=in_specs, out_specs=out_specs, check_vma=False
    )
```

```python
import jax
import jax.numpy as jnp
from jax import lax
from jax.experimental import pallas as pl
from jax.experimental.pallas import tpu as pltpu
from jax.sharding import PartitionSpec as P

def select_blocks(panel_blocks, panel_slots, row_columns, targets):
    partner = jnp.take(panel_slots, row_columns, axis=0)
    width = partner.shape[2]
    match = partner[:, :, :, None] == targets[:, None, None, :]
    found = jnp.any(match, axis=2)
    where_slot = jnp.sum(
        jnp.where(match, jnp.arange(width, dtype=jnp.int32)[None, None, :, None], 0), axis=2
    )
    picked = panel_blocks[row_columns[:, :, None], where_slot]
    return jnp.where(found[:, :, :, None, None], picked, jnp.zeros((), picked.dtype))


def partial_product(row_blocks, row_columns, panel_blocks, panel_slots, targets):
    picked = select_blocks(panel_blocks, panel_slots, row_columns, targets)
    return jnp.einsum("bsxz,bstzy->btxy", row_blocks, picked, preferred_element_type=jnp.float32)


def gather_panel(blocks):
    return lax.all_gather(blocks, "row", axis=0, tiled=True)


def per_device_panels(values, columns):
    rows_here, slots_here, block = (values.shape[0], values.shape[1], values.shape[2])
    row_ids = lax.axis_index("row") * rows_here + jnp.arange(rows_here, dtype=jnp.int32)
    on_diagonal = (columns == row_ids[:, None]).astype(jnp.float32)
    identity = on_diagonal[:, :, None, None] * jnp.eye(block, dtype=jnp.float32)[None, None, :, :]
    panel_blocks = lax.all_gather(values, "row", axis=0, tiled=True)
    panel_slots = lax.all_gather(columns, "row", axis=0, tiled=True)
    row_blocks = lax.all_gather(values, "col", axis=1, tiled=True)
    row_columns = lax.all_gather(columns, "col", axis=1, tiled=True)
    square = partial_product(row_blocks, row_columns, panel_blocks, panel_slots, columns)
    square_low = square.astype(jnp.bfloat16)
    square_panel = gather_panel(square_low)
    square_rows = lax.all_gather(square_low, "col", axis=1, tiled=True)
    fourth = partial_product(square_rows, row_columns, square_panel, panel_slots, columns)
    polynomial = (15.0 * identity - 10.0 * square_low.astype(jnp.float32) + 3.0 * fourth).astype(
        jnp.bfloat16
    )
    polynomial_panel = gather_panel(polynomial)
    updated = (
        partial_product(row_blocks, row_columns, polynomial_panel, panel_slots, columns) * 0.125
    )
    return updated


NEXT = (0, 2, 3, 1)
TILE = 16


def around(array, step, bands):
    return lax.ppermute(array, "row", [(r, (r + 2 * step) % bands) for r in range(bands)])


def across(array, flip):
    return lax.ppermute(array, "col", [(c, c ^ flip) for c in range(4)])


def sibling(array, bands):
    return lax.ppermute(array, "row", [(r, r ^ 1) for r in range(bands)])


def next_flip(flip):
    return jnp.where(flip == 3, 1, flip + 1)


def make_payloads(place, columns, values, first, second):
    size = values.shape[2]
    lane = lax.broadcasted_iota(jnp.int32, (TILE, size), 1)
    line = lax.broadcasted_iota(jnp.int32, (TILE, size), 0)
    tile = jnp.zeros((TILE, size), jnp.int32)
    for m in range(4):
        here = (lane == place[0] + m) & (line == 0)
        tile = jnp.where(here, columns[m // 2, m % 2], tile)
    for t in range(2):
        first[t * size : (t + 1) * size, :] = values[0, t]
        second[t * size : (t + 1) * size, :] = values[1, t]
    second[2 * size :, :] = tile.astype(jnp.float32).astype(jnp.bfloat16)


def local_iteration(origin, *rest):
    lines, planes = rest[:4], rest[4:16]
    out, xs, ys, qs, numbers, pattern, x_table, y_table, near, sem = rest[16:]
    rows, kept, slots, size = 16, 8, 2, 128
    band, c = origin[0], origin[1]
    z, core = lax.div(band, 2), lax.rem(band, 2)
    half = slots * size

    pieces = []
    total = jnp.zeros((TILE, size), jnp.float32)
    for a in range(2):
        long = half + a * TILE
        for source, side in ((lines[a], core), (lines[2 + a], 1 - core)):
            for step in range(4):
                pieces.append((source, step * long, step * 8 + side * 4 + a * 2))
                if a == 1:
                    total += source[step * long + half : step * long + long, :].astype(jnp.float32)
        for group, side in ((planes[a * 3 : a * 3 + 3], core), (planes[6 + a * 3 : 9 + a * 3], 1 - core)):
            for flip in range(3):
                for part in range(2):
                    place = (4 + flip * 2 + part) * 8 + side * 4 + a * 2
                    pieces.append((group[flip], part * half, place))
                if a == 1:
                    total += group[flip][2 * half : 2 * half + TILE, :].astype(jnp.float32)
    numbers[...] = total[0:8].astype(jnp.int32)
    copy = pltpu.make_async_copy(numbers, pattern, sem)
    copy.start()

    nothing = jnp.zeros((size, size), jnp.bfloat16)
    empty = 17 * 8
    xs[empty] = nothing
    ys[rows * kept] = nothing
    qs[rows * slots] = nothing

    def clear(at, carry):
        x_table[at] = empty
        y_table[at] = rows * kept
        return carry

    lax.fori_loop(0, rows * rows, clear, 0, unroll=16)

    for source, first, place in pieces:
        for b in range(slots):
            xs[place + b] = source[first + b * size : first + (b + 1) * size, :]
    for number, piece in enumerate((0, 1, 2, 3, 5, 7, 9)):
        for b in range(8):
            xs[80 + number * 8 + b] = xs[piece * 8 + b].T
    copy.wait()

    def entries(h, g):
        for il in range(4):
            for t in range(slots):
                j = pattern[0, ((h * 2 + il // 2) * 4 + g) * 4 + (il % 2) * slots + t]
                yield 4 * h + il, j, il * slots + t, g * slots + t

    for h in range(4):
        for g in range(4):
            flip = g ^ c
            own = lax.rem(z - h + 4, 4) * 8
            if h == g:
                base = jnp.where(flip == 0, own, (4 + (flip - 1) * 2) * 8)
            else:
                straight = (flip == 0) | (((h ^ c) != 0) & (next_flip(flip) == (h ^ g)))
                base = jnp.where(flip == 0, own, (5 + (flip - 1) * 2) * 8)
                mirror = 80 + jnp.where(flip == 0, own, (3 + flip) * 8)
            for i, j, number, slot in entries(h, g):
                near[i * kept + slot] = j
                y_table[i * rows + j] = i * kept + slot
                if h == g:
                    x_table[i * rows + j] = base + number
            if h != g:

                @pl.when(straight)
                def _():
                    for i, j, number, slot in entries(h, g):
                        x_table[i * rows + j] = base + number
                        x_table[j * rows + i] = mirror + number

    def wide(parts):
        return jnp.concatenate(parts, axis=1)

    def tall(parts):
        return jnp.concatenate(parts, axis=0)

    def dot(left, right):
        return jnp.dot(left, right, preferred_element_type=jnp.float32)

    def x_at(k, j):
        return x_table[k * rows + j]

    def y_at(k, j):
        return y_table[k * rows + j]

    for home in range(4):

        def square(i, carry):
            ks = [near[i * kept + s] for s in range(kept)]
            left = wide([xs[x_at(i, k)] for k in ks])
            js = ks[home * slots :]
            right = tall([wide([xs[x_at(k, j)] for j in js]) for k in ks])
            product = dot(left, right).astype(jnp.bfloat16)
            for t, j in enumerate(js):
                block = product[:, t * size : (t + 1) * size]
                ys[i * kept + home * slots + t] = block
                if t >= slots:
                    ys[y_at(j, i)] = block.T
            return carry

        lax.fori_loop(home * 4, home * 4 + 4, square, 0, unroll=2)

    eye = (
        lax.broadcasted_iota(jnp.int32, (size, size), 0)
        == lax.broadcasted_iota(jnp.int32, (size, size), 1)
    ).astype(jnp.float32)

    def polynomial(i, carry):
        ks = [near[i * kept + s] for s in range(kept)]
        js = [near[i * kept + c * slots + t] for t in range(slots)]
        left = wide([ys[i * kept + s] for s in range(kept)])
        right = tall([wide([ys[y_at(k, j)] for j in js]) for k in ks])
        fourth = dot(left, right)
        for t in range(slots):
            scale = jnp.where(js[t] == i, 15.0, 0.0)
            low = ys[i * kept + c * slots + t].astype(jnp.float32)
            value = scale * eye - 10.0 * low + 3.0 * fourth[:, t * size : (t + 1) * size]
            qs[i * slots + t] = value.astype(jnp.bfloat16)
        return carry

    lax.fori_loop(0, rows, polynomial, 0, unroll=4)

    for a in range(2):
        i = band * 2 + a
        ks = [near[i * kept + s] for s in range(kept)]
        js = [near[i * kept + c * slots + t] for t in range(slots)]

        def q_at(k, j):
            at = y_at(k, j)
            return lax.shift_right_logical(at, 3) * slots + (at & 1)

        left = wide([xs[x_at(i, k)] for k in ks])
        right = tall([wide([qs[q_at(k, j)] for j in js]) for k in ks])
        updated = dot(left, right) * 0.125
        for t in range(slots):
            out[a, t] = updated[:, t * size : (t + 1) * size]


def per_device_whole(values, columns):
    bands = lax.axis_size("row")
    size = values.shape[2]
    band, c = lax.axis_index("row"), lax.axis_index("col")
    z = band // 2
    place = ((band * 4 + c) * 4).reshape(1).astype(jnp.int32)
    mine = pl.pallas_call(
        make_payloads,
        out_shape=[
            jax.ShapeDtypeStruct((2 * size, size), jnp.bfloat16),
            jax.ShapeDtypeStruct((2 * size + TILE, size), jnp.bfloat16),
        ],
        in_specs=[
            pl.BlockSpec(memory_space=pltpu.SMEM),
            pl.BlockSpec(memory_space=pltpu.SMEM),
            pl.BlockSpec(memory_space=pltpu.VMEM),
        ],
        out_specs=[pl.BlockSpec(memory_space=pltpu.VMEM)] * 2,
    )(place, columns, values)

    def from_line(line, h):
        return lax.dynamic_index_in_dim(line, (z - h) % 4, axis=0, keepdims=False)

    lines = [
        jnp.stack([half] + [around(half, step, bands) for step in range(1, 4)]) for half in mine
    ]
    here, lines_there = [], []
    for a, line in enumerate(lines):
        tail = [jnp.sum(line[:, 2 * size :], axis=0)] if a else []
        for flip in range(1, 4):
            parts = [from_line(line, h)[: 2 * size] for h in (c, c ^ NEXT[flip])]
            here.append(across(jnp.concatenate(parts + tail), flip))
        lines_there.append(sibling(line.reshape(-1, size), bands))
    there = [sibling(piece, bands) for piece in here]
    lines = [line.reshape(-1, size) for line in lines]
    origin = jnp.stack([band, c]).astype(jnp.int32)
    return pl.pallas_call(
        local_iteration,
        out_shape=jax.ShapeDtypeStruct(values.shape, jnp.float32),
        in_specs=[pl.BlockSpec(memory_space=pltpu.SMEM)]
        + [pl.BlockSpec(memory_space=pltpu.VMEM)] * 16,
        out_specs=pl.BlockSpec(memory_space=pltpu.VMEM),
        scratch_shapes=[
            pltpu.VMEM((17 * 8 + 1, size, size), jnp.bfloat16),
            pltpu.VMEM((129, size, size), jnp.bfloat16),
            pltpu.VMEM((33, size, size), jnp.bfloat16),
            pltpu.VMEM((8, size), jnp.int32),
            pltpu.SMEM((8, size), jnp.int32),
            pltpu.SMEM((256,), jnp.int32),
            pltpu.SMEM((256,), jnp.int32),
            pltpu.SMEM((128,), jnp.int32),
            pltpu.SemaphoreType.DMA,
        ],
        compiler_params=pltpu.CompilerParams(vmem_limit_bytes=32 * 1024 * 1024),
    )(origin, *lines, *lines_there, *here, *there)


def per_device(values, columns):
    sizes = (lax.axis_size("row"), lax.axis_size("col"), *values.shape)
    if sizes == (8, 4, 2, 2, 128, 128):
        return per_device_whole(values, columns)
    return per_device_panels(values, columns)


def solution(mesh):
    in_specs = (P("row", "col", None, None), P("row", "col"))
    out_specs = P("row", "col", None, None)
    return jax.shard_map(
        per_device, mesh=mesh, in_specs=in_specs, out_specs=out_specs, check_vma=False
    )
```

```python
import jax
import jax.numpy as jnp
from jax import lax
from jax.experimental import pallas as pl
from jax.experimental.pallas import tpu as pltpu
from jax.sharding import PartitionSpec as P

def select_blocks(panel_blocks, panel_slots, row_columns, targets):
    partner = jnp.take(panel_slots, row_columns, axis=0)
    width = partner.shape[2]
    match = partner[:, :, :, None] == targets[:, None, None, :]
    found = jnp.any(match, axis=2)
    where_slot = jnp.sum(
        jnp.where(match, jnp.arange(width, dtype=jnp.int32)[None, None, :, None], 0), axis=2
    )
    picked = panel_blocks[row_columns[:, :, None], where_slot]
    return jnp.where(found[:, :, :, None, None], picked, jnp.zeros((), picked.dtype))


def partial_product(row_blocks, row_columns, panel_blocks, panel_slots, targets):
    picked = select_blocks(panel_blocks, panel_slots, row_columns, targets)
    return jnp.einsum("bsxz,bstzy->btxy", row_blocks, picked, preferred_element_type=jnp.float32)


def gather_panel(blocks):
    return lax.all_gather(blocks, "row", axis=0, tiled=True)


def per_device_panels(values, columns):
    rows_here, slots_here, block = (values.shape[0], values.shape[1], values.shape[2])
    row_ids = lax.axis_index("row") * rows_here + jnp.arange(rows_here, dtype=jnp.int32)
    on_diagonal = (columns == row_ids[:, None]).astype(jnp.float32)
    identity = on_diagonal[:, :, None, None] * jnp.eye(block, dtype=jnp.float32)[None, None, :, :]
    panel_blocks = lax.all_gather(values, "row", axis=0, tiled=True)
    panel_slots = lax.all_gather(columns, "row", axis=0, tiled=True)
    row_blocks = lax.all_gather(values, "col", axis=1, tiled=True)
    row_columns = lax.all_gather(columns, "col", axis=1, tiled=True)
    square = partial_product(row_blocks, row_columns, panel_blocks, panel_slots, columns)
    square_low = square.astype(jnp.bfloat16)
    square_panel = gather_panel(square_low)
    square_rows = lax.all_gather(square_low, "col", axis=1, tiled=True)
    fourth = partial_product(square_rows, row_columns, square_panel, panel_slots, columns)
    polynomial = (15.0 * identity - 10.0 * square_low.astype(jnp.float32) + 3.0 * fourth).astype(
        jnp.bfloat16
    )
    polynomial_panel = gather_panel(polynomial)
    updated = (
        partial_product(row_blocks, row_columns, polynomial_panel, panel_slots, columns) * 0.125
    )
    return updated


NEXT = (0, 2, 3, 1)
TILE = 16


def around(array, step, bands):
    return lax.ppermute(array, "row", [(r, (r + 2 * step) % bands) for r in range(bands)])


def across(array, flip):
    return lax.ppermute(array, "col", [(c, c ^ flip) for c in range(4)])


def sibling(array, bands):
    return lax.ppermute(array, "row", [(r, r ^ 1) for r in range(bands)])


def next_flip(flip):
    return jnp.where(flip == 3, 1, flip + 1)


def make_tile(place, columns, out):
    lane = lax.broadcasted_iota(jnp.int32, out.shape, 1)
    line = lax.broadcasted_iota(jnp.int32, out.shape, 0)
    tile = jnp.zeros(out.shape, jnp.int32)
    for m in range(4):
        here = (lane == place[0] + m) & (line == 0)
        tile = jnp.where(here, columns[m // 2, m % 2], tile)
    out[...] = tile.astype(jnp.float32).astype(jnp.bfloat16)


def local_iteration(origin, *rest):
    lines, planes = rest[:2], (rest[2:5], rest[5:8])
    out, xs, ys, qs, numbers, pattern, x_table, y_table, near, sem = rest[8:]
    rows, kept, slots, size = 16, 8, 2, 128
    band, c = origin[0], origin[1]
    z, core = lax.div(band, 2), lax.rem(band, 2)
    part_rows = 4 * size

    pieces = []
    total = jnp.zeros((TILE, size), jnp.float32)
    for line, group, side in zip(lines, planes, (core, 1 - core)):
        for step in range(4):
            pieces.append((line, step * part_rows, step * 8 + side * 4))
        total += line[4 * part_rows :, :].astype(jnp.float32)
        for flip in range(3):
            for part in range(2):
                place = (4 + flip * 2 + part) * 8 + side * 4
                pieces.append((group[flip], part * part_rows, place))
            total += group[flip][2 * part_rows :, :].astype(jnp.float32)
    numbers[...] = total[0:8].astype(jnp.int32)
    copy = pltpu.make_async_copy(numbers, pattern, sem)
    copy.start()

    nothing = jnp.zeros((size, size), jnp.bfloat16)
    empty = 17 * 8
    xs[empty] = nothing
    ys[rows * kept] = nothing
    qs[rows * slots] = nothing

    def clear(at, carry):
        x_table[at] = empty
        y_table[at] = rows * kept
        return carry

    lax.fori_loop(0, rows * rows, clear, 0, unroll=16)

    for source, first, place in pieces:
        for b in range(4):
            xs[place + b] = source[first + b * size : first + (b + 1) * size, :]
    for number, piece in enumerate((0, 1, 2, 3, 5, 7, 9)):
        for b in range(8):
            xs[80 + number * 8 + b] = xs[piece * 8 + b].T
    copy.wait()

    def entries(h, g):
        for il in range(4):
            for t in range(slots):
                j = pattern[0, ((h * 2 + il // 2) * 4 + g) * 4 + (il % 2) * slots + t]
                yield 4 * h + il, j, il * slots + t, g * slots + t

    for h in range(4):
        for g in range(4):
            flip = g ^ c
            own = lax.rem(z - h + 4, 4) * 8
            if h == g:
                base = jnp.where(flip == 0, own, (4 + (flip - 1) * 2) * 8)
            else:
                straight = (flip == 0) | (((h ^ c) != 0) & (next_flip(flip) == (h ^ g)))
                base = jnp.where(flip == 0, own, (5 + (flip - 1) * 2) * 8)
                mirror = 80 + jnp.where(flip == 0, own, (3 + flip) * 8)
            for i, j, number, slot in entries(h, g):
                near[i * kept + slot] = j
                y_table[i * rows + j] = i * kept + slot
                if h == g:
                    x_table[i * rows + j] = base + number
            if h != g:

                @pl.when(straight)
                def _():
                    for i, j, number, slot in entries(h, g):
                        x_table[i * rows + j] = base + number
                        x_table[j * rows + i] = mirror + number

    def wide(parts):
        return jnp.concatenate(parts, axis=1)

    def tall(parts):
        return jnp.concatenate(parts, axis=0)

    def dot(left, right):
        return jnp.dot(left, right, preferred_element_type=jnp.float32)

    def x_at(k, j):
        return x_table[k * rows + j]

    def y_at(k, j):
        return y_table[k * rows + j]

    for home in range(4):

        def square(i, carry):
            ks = [near[i * kept + s] for s in range(kept)]
            left = wide([xs[x_at(i, k)] for k in ks])
            js = ks[home * slots :]
            right = tall([wide([xs[x_at(k, j)] for j in js]) for k in ks])
            product = dot(left, right).astype(jnp.bfloat16)
            for t, j in enumerate(js):
                block = product[:, t * size : (t + 1) * size]
                ys[i * kept + home * slots + t] = block
                if t >= slots:
                    ys[y_at(j, i)] = block.T
            return carry

        lax.fori_loop(home * 4, home * 4 + 4, square, 0, unroll=4)

    eye = (
        lax.broadcasted_iota(jnp.int32, (size, size), 0)
        == lax.broadcasted_iota(jnp.int32, (size, size), 1)
    ).astype(jnp.float32)

    def polynomial(i, carry):
        ks = [near[i * kept + s] for s in range(kept)]
        js = [near[i * kept + c * slots + t] for t in range(slots)]
        left = wide([ys[i * kept + s] for s in range(kept)])
        right = tall([wide([ys[y_at(k, j)] for j in js]) for k in ks])
        fourth = dot(left, right)
        for t in range(slots):
            scale = jnp.where(js[t] == i, 15.0, 0.0)
            low = ys[i * kept + c * slots + t].astype(jnp.float32)
            value = scale * eye - 10.0 * low + 3.0 * fourth[:, t * size : (t + 1) * size]
            qs[i * slots + t] = value.astype(jnp.bfloat16)
        return carry

    lax.fori_loop(0, rows, polynomial, 0, unroll=8)

    for a in range(2):
        i = band * 2 + a
        ks = [near[i * kept + s] for s in range(kept)]
        js = [near[i * kept + c * slots + t] for t in range(slots)]

        def q_at(k, j):
            at = y_at(k, j)
            return lax.shift_right_logical(at, 3) * slots + (at & 1)

        left = wide([xs[x_at(i, k)] for k in ks])
        right = tall([wide([qs[q_at(k, j)] for j in js]) for k in ks])
        updated = dot(left, right) * 0.125
        for t in range(slots):
            out[a, t] = updated[:, t * size : (t + 1) * size]


def per_device_whole(values, columns):
    bands = lax.axis_size("row")
    size = values.shape[2]
    band, c = lax.axis_index("row"), lax.axis_index("col")
    z = band // 2
    place = ((band * 4 + c) * 4).reshape(1).astype(jnp.int32)
    smem, vmem = pl.BlockSpec(memory_space=pltpu.SMEM), pl.BlockSpec(memory_space=pltpu.VMEM)
    mine = values.reshape(4 * size, size)
    line = [mine] + [around(mine, step, bands) for step in range(1, 4)]
    tile = pl.pallas_call(
        make_tile,
        out_shape=jax.ShapeDtypeStruct((TILE, size), jnp.bfloat16),
        in_specs=[smem, smem],
        out_specs=vmem,
    )(place, columns)
    tile = tile + sum(around(tile, step, bands) for step in range(1, 4))
    stacked = jnp.stack(line)

    def from_line(h):
        return lax.dynamic_index_in_dim(stacked, (z - h) % 4, axis=0, keepdims=False)

    here = []
    for flip in range(1, 4):
        parts = [from_line(h) for h in (c, c ^ NEXT[flip])]
        here.append(across(jnp.concatenate(parts + [tile]), flip))
    line = jnp.concatenate(line + [tile])
    line_there = sibling(line, bands)
    there = [sibling(piece, bands) for piece in here]
    origin = jnp.stack([band, c]).astype(jnp.int32)
    return pl.pallas_call(
        local_iteration,
        out_shape=jax.ShapeDtypeStruct(values.shape, jnp.float32),
        in_specs=[smem] + [vmem] * 8,
        out_specs=vmem,
        scratch_shapes=[
            pltpu.VMEM((17 * 8 + 1, size, size), jnp.bfloat16),
            pltpu.VMEM((129, size, size), jnp.bfloat16),
            pltpu.VMEM((33, size, size), jnp.bfloat16),
            pltpu.VMEM((8, size), jnp.int32),
            pltpu.SMEM((8, size), jnp.int32),
            pltpu.SMEM((256,), jnp.int32),
            pltpu.SMEM((256,), jnp.int32),
            pltpu.SMEM((128,), jnp.int32),
            pltpu.SemaphoreType.DMA,
        ],
        compiler_params=pltpu.CompilerParams(vmem_limit_bytes=32 * 1024 * 1024),
    )(origin, line, line_there, *here, *there)


def per_device(values, columns):
    sizes = (lax.axis_size("row"), lax.axis_size("col"), *values.shape)
    if sizes == (8, 4, 2, 2, 128, 128):
        return per_device_whole(values, columns)
    return per_device_panels(values, columns)


def solution(mesh):
    in_specs = (P("row", "col", None, None), P("row", "col"))
    out_specs = P("row", "col", None, None)
    return jax.shard_map(
        per_device, mesh=mesh, in_specs=in_specs, out_specs=out_specs, check_vma=False
    )
```

```python
import jax
import jax.numpy as jnp
from jax import lax
from jax.experimental import pallas as pl
from jax.experimental.pallas import tpu as pltpu
from jax.sharding import PartitionSpec as P

def select_blocks(panel_blocks, panel_slots, row_columns, targets):
    partner = jnp.take(panel_slots, row_columns, axis=0)
    width = partner.shape[2]
    match = partner[:, :, :, None] == targets[:, None, None, :]
    found = jnp.any(match, axis=2)
    where_slot = jnp.sum(
        jnp.where(match, jnp.arange(width, dtype=jnp.int32)[None, None, :, None], 0), axis=2
    )
    picked = panel_blocks[row_columns[:, :, None], where_slot]
    return jnp.where(found[:, :, :, None, None], picked, jnp.zeros((), picked.dtype))


def partial_product(row_blocks, row_columns, panel_blocks, panel_slots, targets):
    picked = select_blocks(panel_blocks, panel_slots, row_columns, targets)
    return jnp.einsum("bsxz,bstzy->btxy", row_blocks, picked, preferred_element_type=jnp.float32)


def gather_panel(blocks):
    return lax.all_gather(blocks, "row", axis=0, tiled=True)


def per_device_panels(values, columns):
    rows_here, slots_here, block = (values.shape[0], values.shape[1], values.shape[2])
    row_ids = lax.axis_index("row") * rows_here + jnp.arange(rows_here, dtype=jnp.int32)
    on_diagonal = (columns == row_ids[:, None]).astype(jnp.float32)
    identity = on_diagonal[:, :, None, None] * jnp.eye(block, dtype=jnp.float32)[None, None, :, :]
    panel_blocks = lax.all_gather(values, "row", axis=0, tiled=True)
    panel_slots = lax.all_gather(columns, "row", axis=0, tiled=True)
    row_blocks = lax.all_gather(values, "col", axis=1, tiled=True)
    row_columns = lax.all_gather(columns, "col", axis=1, tiled=True)
    square = partial_product(row_blocks, row_columns, panel_blocks, panel_slots, columns)
    square_low = square.astype(jnp.bfloat16)
    square_panel = gather_panel(square_low)
    square_rows = lax.all_gather(square_low, "col", axis=1, tiled=True)
    fourth = partial_product(square_rows, row_columns, square_panel, panel_slots, columns)
    polynomial = (15.0 * identity - 10.0 * square_low.astype(jnp.float32) + 3.0 * fourth).astype(
        jnp.bfloat16
    )
    polynomial_panel = gather_panel(polynomial)
    updated = (
        partial_product(row_blocks, row_columns, polynomial_panel, panel_slots, columns) * 0.125
    )
    return updated


NEXT = (0, 2, 3, 1)
TILE = 16


def around(array, step, bands):
    return lax.ppermute(array, "row", [(r, (r + 2 * step) % bands) for r in range(bands)])


def across(array, flip):
    return lax.ppermute(array, "col", [(c, c ^ flip) for c in range(4)])


def sibling(array, bands):
    return lax.ppermute(array, "row", [(r, r ^ 1) for r in range(bands)])


def next_flip(flip):
    return jnp.where(flip == 3, 1, flip + 1)


def make_tile(place, columns, out):
    lane = lax.broadcasted_iota(jnp.int32, out.shape, 1)
    line = lax.broadcasted_iota(jnp.int32, out.shape, 0)
    tile = jnp.zeros(out.shape, jnp.int32)
    for m in range(4):
        here = (lane == place[0] + m) & (line == 0)
        tile = jnp.where(here, columns[m // 2, m % 2], tile)
    out[...] = tile.astype(jnp.float32).astype(jnp.bfloat16)


def local_iteration(origin, *rest):
    lines, planes = rest[:2], (rest[2:5], rest[5:8])
    out, xs, ys, qs, numbers, pattern, x_table, y_table, near, sem = rest[8:]
    rows, kept, slots, size = 16, 8, 2, 128
    band, c = origin[0], origin[1]
    z, core = lax.div(band, 2), lax.rem(band, 2)
    part_rows = 4 * size

    pieces = []
    total = jnp.zeros((TILE, size), jnp.float32)
    for line, group, side in zip(lines, planes, (core, 1 - core)):
        for step in range(4):
            pieces.append((line, step * part_rows, step * 8 + side * 4))
        total += line[4 * part_rows :, :].astype(jnp.float32)
        for flip in range(3):
            for part in range(2):
                place = (4 + flip * 2 + part) * 8 + side * 4
                pieces.append((group[flip], part * part_rows, place))
            total += group[flip][2 * part_rows :, :].astype(jnp.float32)
    numbers[...] = total[0:8].astype(jnp.int32)
    copy = pltpu.make_async_copy(numbers, pattern, sem)
    copy.start()

    nothing = jnp.zeros((size, size), jnp.bfloat16)
    empty = 17 * 8
    xs[empty] = nothing
    ys[rows * kept] = nothing
    qs[rows * slots] = nothing

    def clear(at, carry):
        x_table[at] = empty
        y_table[at] = rows * kept
        return carry

    lax.fori_loop(0, rows * rows, clear, 0, unroll=16)

    for source, first, place in pieces:
        for b in range(4):
            xs[place + b] = source[first + b * size : first + (b + 1) * size, :]
    copy.wait()

    def entries(h, g):
        for il in range(4):
            for t in range(slots):
                j = pattern[0, ((h * 2 + il // 2) * 4 + g) * 4 + (il % 2) * slots + t]
                yield 4 * h + il, j, il * slots + t, g * slots + t

    for h in range(4):
        for g in range(4):
            flip = g ^ c
            own = lax.rem(z - h + 4, 4) * 8
            if h == g:
                base = jnp.where(flip == 0, own, (4 + (flip - 1) * 2) * 8)
            else:
                straight = (flip == 0) | (((h ^ c) != 0) & (next_flip(flip) == (h ^ g)))
                base = jnp.where(flip == 0, own, (5 + (flip - 1) * 2) * 8)
                mirror = 80 + jnp.where(flip == 0, own, (3 + flip) * 8)
            for i, j, number, slot in entries(h, g):
                near[i * kept + slot] = j
                y_table[i * rows + j] = i * kept + slot
                if h == g:
                    x_table[i * rows + j] = base + number
            if h != g:
                unused = jnp.where(straight, 0, rows * rows)
                for i, j, number, slot in entries(h, g):
                    x_table[unused + i * rows + j] = base + number
                    x_table[unused + j * rows + i] = mirror + number

    for number, piece in enumerate((0, 1, 2, 3, 5, 7, 9)):
        for b in range(8):
            xs[80 + number * 8 + b] = xs[piece * 8 + b].T

    def wide(parts):
        return jnp.concatenate(parts, axis=1)

    def tall(parts):
        return jnp.concatenate(parts, axis=0)

    def dot(left, right):
        return jnp.dot(left, right, preferred_element_type=jnp.float32)

    def x_at(k, j):
        return x_table[k * rows + j]

    def y_at(k, j):
        return y_table[k * rows + j]

    for home in range(4):

        def square(i, carry):
            ks = [near[i * kept + s] for s in range(kept)]
            left = wide([xs[x_at(i, k)] for k in ks])
            js = ks[home * slots :]
            right = tall([wide([xs[x_at(k, j)] for j in js]) for k in ks])
            product = dot(left, right).astype(jnp.bfloat16)
            for t, j in enumerate(js):
                block = product[:, t * size : (t + 1) * size]
                ys[i * kept + home * slots + t] = block
                if t >= slots:
                    ys[y_at(j, i)] = block.T
            return carry

        lax.fori_loop(home * 4, home * 4 + 4, square, 0, unroll=4)

    eye = (
        lax.broadcasted_iota(jnp.int32, (size, size), 0)
        == lax.broadcasted_iota(jnp.int32, (size, size), 1)
    ).astype(jnp.float32)

    def polynomial(i, carry):
        ks = [near[i * kept + s] for s in range(kept)]
        js = [near[i * kept + c * slots + t] for t in range(slots)]
        left = wide([ys[i * kept + s] for s in range(kept)])
        right = tall([wide([ys[y_at(k, j)] for j in js]) for k in ks])
        fourth = dot(left, right)
        for t in range(slots):
            scale = jnp.where(js[t] == i, 15.0, 0.0)
            low = ys[i * kept + c * slots + t].astype(jnp.float32)
            value = scale * eye - 10.0 * low + 3.0 * fourth[:, t * size : (t + 1) * size]
            qs[i * slots + t] = value.astype(jnp.bfloat16)
        return carry

    lax.fori_loop(0, rows, polynomial, 0, unroll=16)

    for a in range(2):
        i = band * 2 + a
        ks = [near[i * kept + s] for s in range(kept)]
        js = [near[i * kept + c * slots + t] for t in range(slots)]

        def q_at(k, j):
            at = y_at(k, j)
            return lax.shift_right_logical(at, 3) * slots + (at & 1)

        left = wide([xs[x_at(i, k)] for k in ks])
        right = tall([wide([qs[q_at(k, j)] for j in js]) for k in ks])
        updated = dot(left, right) * 0.125
        for t in range(slots):
            out[a, t] = updated[:, t * size : (t + 1) * size]


def per_device_whole(values, columns):
    bands = lax.axis_size("row")
    size = values.shape[2]
    band, c = lax.axis_index("row"), lax.axis_index("col")
    z = band // 2
    place = ((band * 4 + c) * 4).reshape(1).astype(jnp.int32)
    smem, vmem = pl.BlockSpec(memory_space=pltpu.SMEM), pl.BlockSpec(memory_space=pltpu.VMEM)
    mine = values.reshape(4 * size, size)
    line = [mine] + [around(mine, step, bands) for step in range(1, 4)]
    tile = pl.pallas_call(
        make_tile,
        out_shape=jax.ShapeDtypeStruct((TILE, size), jnp.bfloat16),
        in_specs=[smem, smem],
        out_specs=vmem,
    )(place, columns)
    tile = tile + sum(around(tile, step, bands) for step in range(1, 4))
    stacked = jnp.stack(line)

    def from_line(h):
        return lax.dynamic_index_in_dim(stacked, (z - h) % 4, axis=0, keepdims=False)

    here = []
    for flip in range(1, 4):
        parts = [from_line(h) for h in (c, c ^ NEXT[flip])]
        here.append(across(jnp.concatenate(parts + [tile]), flip))
    line = jnp.concatenate(line + [tile])
    line_there = sibling(line, bands)
    there = [sibling(piece, bands) for piece in here]
    origin = jnp.stack([band, c]).astype(jnp.int32)
    return pl.pallas_call(
        local_iteration,
        out_shape=jax.ShapeDtypeStruct(values.shape, jnp.float32),
        in_specs=[smem] + [vmem] * 8,
        out_specs=vmem,
        scratch_shapes=[
            pltpu.VMEM((17 * 8 + 1, size, size), jnp.bfloat16),
            pltpu.VMEM((129, size, size), jnp.bfloat16),
            pltpu.VMEM((33, size, size), jnp.bfloat16),
            pltpu.VMEM((8, size), jnp.int32),
            pltpu.SMEM((8, size), jnp.int32),
            pltpu.SMEM((512,), jnp.int32),
            pltpu.SMEM((256,), jnp.int32),
            pltpu.SMEM((128,), jnp.int32),
            pltpu.SemaphoreType.DMA,
        ],
        compiler_params=pltpu.CompilerParams(vmem_limit_bytes=32 * 1024 * 1024),
    )(origin, line, line_there, *here, *there)


def per_device(values, columns):
    sizes = (lax.axis_size("row"), lax.axis_size("col"), *values.shape)
    if sizes == (8, 4, 2, 2, 128, 128):
        return per_device_whole(values, columns)
    return per_device_panels(values, columns)


def solution(mesh):
    in_specs = (P("row", "col", None, None), P("row", "col"))
    out_specs = P("row", "col", None, None)
    return jax.shard_map(
        per_device, mesh=mesh, in_specs=in_specs, out_specs=out_specs, check_vma=False
    )
```

```python
import jax
import jax.numpy as jnp
from jax import lax
from jax.experimental import pallas as pl
from jax.experimental.pallas import tpu as pltpu
from jax.sharding import PartitionSpec as P

def select_blocks(panel_blocks, panel_slots, row_columns, targets):
    partner = jnp.take(panel_slots, row_columns, axis=0)
    width = partner.shape[2]
    match = partner[:, :, :, None] == targets[:, None, None, :]
    found = jnp.any(match, axis=2)
    where_slot = jnp.sum(
        jnp.where(match, jnp.arange(width, dtype=jnp.int32)[None, None, :, None], 0), axis=2
    )
    picked = panel_blocks[row_columns[:, :, None], where_slot]
    return jnp.where(found[:, :, :, None, None], picked, jnp.zeros((), picked.dtype))


def partial_product(row_blocks, row_columns, panel_blocks, panel_slots, targets):
    picked = select_blocks(panel_blocks, panel_slots, row_columns, targets)
    return jnp.einsum("bsxz,bstzy->btxy", row_blocks, picked, preferred_element_type=jnp.float32)


def gather_panel(blocks):
    return lax.all_gather(blocks, "row", axis=0, tiled=True)


def per_device_panels(values, columns):
    rows_here, slots_here, block = (values.shape[0], values.shape[1], values.shape[2])
    row_ids = lax.axis_index("row") * rows_here + jnp.arange(rows_here, dtype=jnp.int32)
    on_diagonal = (columns == row_ids[:, None]).astype(jnp.float32)
    identity = on_diagonal[:, :, None, None] * jnp.eye(block, dtype=jnp.float32)[None, None, :, :]
    panel_blocks = lax.all_gather(values, "row", axis=0, tiled=True)
    panel_slots = lax.all_gather(columns, "row", axis=0, tiled=True)
    row_blocks = lax.all_gather(values, "col", axis=1, tiled=True)
    row_columns = lax.all_gather(columns, "col", axis=1, tiled=True)
    square = partial_product(row_blocks, row_columns, panel_blocks, panel_slots, columns)
    square_low = square.astype(jnp.bfloat16)
    square_panel = gather_panel(square_low)
    square_rows = lax.all_gather(square_low, "col", axis=1, tiled=True)
    fourth = partial_product(square_rows, row_columns, square_panel, panel_slots, columns)
    polynomial = (15.0 * identity - 10.0 * square_low.astype(jnp.float32) + 3.0 * fourth).astype(
        jnp.bfloat16
    )
    polynomial_panel = gather_panel(polynomial)
    updated = (
        partial_product(row_blocks, row_columns, polynomial_panel, panel_slots, columns) * 0.125
    )
    return updated


NEXT = (0, 2, 3, 1)
TILE = 16


def around(array, step, bands):
    return lax.ppermute(array, "row", [(r, (r + 2 * step) % bands) for r in range(bands)])


def across(array, flip):
    return lax.ppermute(array, "col", [(c, c ^ flip) for c in range(4)])


def sibling(array, bands):
    return lax.ppermute(array, "row", [(r, r ^ 1) for r in range(bands)])


def next_flip(flip):
    return jnp.where(flip == 3, 1, flip + 1)


def make_tile(place, columns, out):
    lane = lax.broadcasted_iota(jnp.int32, out.shape, 1)
    line = lax.broadcasted_iota(jnp.int32, out.shape, 0)
    tile = jnp.zeros(out.shape, jnp.int32)
    for m in range(4):
        here = (lane == place[0] + m) & (line == 0)
        tile = jnp.where(here, columns[m // 2, m % 2], tile)
    out[...] = tile.astype(jnp.float32).astype(jnp.bfloat16)


def mirror_line(line, out):
    size = out.shape[1]
    for step in range(4):
        for b in range(4):
            out[step * 4 + b] = line[step, b * size : (b + 1) * size, :].T


def local_iteration(origin, *rest):
    lines, planes = rest[:2], (rest[2:5], rest[5:8])
    out, xs, ys, qs, numbers, pattern, x_table, y_table, near, sem = rest[9:]
    mirrored = rest[8]
    rows, kept, slots, size = 16, 8, 2, 128
    band, c = origin[0], origin[1]
    z, core = lax.div(band, 2), lax.rem(band, 2)
    part_rows = 4 * size

    pieces = []
    total = jnp.zeros((TILE, size), jnp.float32)
    for line, group, side in zip(lines, planes, (core, 1 - core)):
        for step in range(4):
            pieces.append((line, step * part_rows, step * 8 + side * 4))
        total += line[4 * part_rows :, :].astype(jnp.float32)
        for flip in range(3):
            for part in range(2):
                place = (4 + flip * 2 + part) * 8 + side * 4
                pieces.append((group[flip], part * part_rows, place))
            total += group[flip][2 * part_rows :, :].astype(jnp.float32)
    numbers[...] = total[0:8].astype(jnp.int32)
    copy = pltpu.make_async_copy(numbers, pattern, sem)
    copy.start()

    nothing = jnp.zeros((size, size), jnp.bfloat16)
    empty = 17 * 8
    xs[empty] = nothing
    ys[rows * kept] = nothing
    qs[rows * slots] = nothing

    def clear(at, carry):
        x_table[at] = empty
        y_table[at] = rows * kept
        return carry

    lax.fori_loop(0, rows * rows, clear, 0, unroll=16)

    for source, first, place in pieces:
        for b in range(4):
            xs[place + b] = source[first + b * size : first + (b + 1) * size, :]
    copy.wait()

    def entries(h, g):
        for il in range(4):
            for t in range(slots):
                j = pattern[0, ((h * 2 + il // 2) * 4 + g) * 4 + (il % 2) * slots + t]
                yield 4 * h + il, j, il * slots + t, g * slots + t

    for h in range(4):
        for g in range(4):
            flip = g ^ c
            own = lax.rem(z - h + 4, 4) * 8
            if h == g:
                base = jnp.where(flip == 0, own, (4 + (flip - 1) * 2) * 8)
            else:
                straight = (flip == 0) | (((h ^ c) != 0) & (next_flip(flip) == (h ^ g)))
                base = jnp.where(flip == 0, own, (5 + (flip - 1) * 2) * 8)
                mirror = 80 + jnp.where(flip == 0, own, (3 + flip) * 8)
            for i, j, number, slot in entries(h, g):
                near[i * kept + slot] = j
                y_table[i * rows + j] = i * kept + slot
                if h == g:
                    x_table[i * rows + j] = base + number
            if h != g:
                unused = jnp.where(straight, 0, rows * rows)
                for i, j, number, slot in entries(h, g):
                    x_table[unused + i * rows + j] = base + number
                    x_table[unused + j * rows + i] = mirror + number

    for step in range(4):
        for b in range(4):
            first = step * part_rows + b * size
            xs[80 + step * 8 + core * 4 + b] = mirrored[step * 4 + b]
            xs[80 + step * 8 + (1 - core) * 4 + b] = lines[1][first : first + size, :].T
    for number, piece in enumerate((5, 7, 9)):
        for b in range(8):
            xs[112 + number * 8 + b] = xs[piece * 8 + b].T

    def wide(parts):
        return jnp.concatenate(parts, axis=1)

    def tall(parts):
        return jnp.concatenate(parts, axis=0)

    def dot(left, right):
        return jnp.dot(left, right, preferred_element_type=jnp.float32)

    def x_at(k, j):
        return x_table[k * rows + j]

    def y_at(k, j):
        return y_table[k * rows + j]

    for home in range(4):

        def square(i, carry):
            ks = [near[i * kept + s] for s in range(kept)]
            left = wide([xs[x_at(i, k)] for k in ks])
            js = ks[home * slots :]
            right = tall([wide([xs[x_at(k, j)] for j in js]) for k in ks])
            product = dot(left, right).astype(jnp.bfloat16)
            for t, j in enumerate(js):
                block = product[:, t * size : (t + 1) * size]
                ys[i * kept + home * slots + t] = block
                if t >= slots:
                    ys[y_at(j, i)] = block.T
            return carry

        lax.fori_loop(home * 4, home * 4 + 4, square, 0, unroll=4)

    eye = (
        lax.broadcasted_iota(jnp.int32, (size, size), 0)
        == lax.broadcasted_iota(jnp.int32, (size, size), 1)
    ).astype(jnp.float32)

    def polynomial(i, carry):
        ks = [near[i * kept + s] for s in range(kept)]
        js = [near[i * kept + c * slots + t] for t in range(slots)]
        left = wide([ys[i * kept + s] for s in range(kept)])
        right = tall([wide([ys[y_at(k, j)] for j in js]) for k in ks])
        fourth = dot(left, right)
        for t in range(slots):
            scale = jnp.where(js[t] == i, 15.0, 0.0)
            low = ys[i * kept + c * slots + t].astype(jnp.float32)
            value = scale * eye - 10.0 * low + 3.0 * fourth[:, t * size : (t + 1) * size]
            qs[i * slots + t] = value.astype(jnp.bfloat16)
        return carry

    lax.fori_loop(0, rows, polynomial, 0, unroll=16)

    for a in range(2):
        i = band * 2 + a
        ks = [near[i * kept + s] for s in range(kept)]
        js = [near[i * kept + c * slots + t] for t in range(slots)]

        def q_at(k, j):
            at = y_at(k, j)
            return lax.shift_right_logical(at, 3) * slots + (at & 1)

        left = wide([xs[x_at(i, k)] for k in ks])
        right = tall([wide([qs[q_at(k, j)] for j in js]) for k in ks])
        updated = dot(left, right) * 0.125
        for t in range(slots):
            out[a, t] = updated[:, t * size : (t + 1) * size]


def per_device_whole(values, columns):
    bands = lax.axis_size("row")
    size = values.shape[2]
    band, c = lax.axis_index("row"), lax.axis_index("col")
    z = band // 2
    place = ((band * 4 + c) * 4).reshape(1).astype(jnp.int32)
    smem, vmem = pl.BlockSpec(memory_space=pltpu.SMEM), pl.BlockSpec(memory_space=pltpu.VMEM)
    mine = values.reshape(4 * size, size)
    line = [mine] + [around(mine, step, bands) for step in range(1, 4)]
    tile = pl.pallas_call(
        make_tile,
        out_shape=jax.ShapeDtypeStruct((TILE, size), jnp.bfloat16),
        in_specs=[smem, smem],
        out_specs=vmem,
    )(place, columns)
    tile = tile + sum(around(tile, step, bands) for step in range(1, 4))
    stacked = jnp.stack(line)

    def from_line(h):
        return lax.dynamic_index_in_dim(stacked, (z - h) % 4, axis=0, keepdims=False)

    here = []
    for flip in range(1, 4):
        parts = [from_line(h) for h in (c, c ^ NEXT[flip])]
        here.append(across(jnp.concatenate(parts + [tile]), flip))
    line = jnp.concatenate(line + [tile])
    line_there = sibling(line, bands)
    mirrored = pl.pallas_call(
        mirror_line,
        out_shape=jax.ShapeDtypeStruct((16, size, size), jnp.bfloat16),
        in_specs=[vmem],
        out_specs=vmem,
    )(stacked)
    mirrored, *here = lax.optimization_barrier((mirrored, *here))
    there = [sibling(piece, bands) for piece in here]
    origin = jnp.stack([band, c]).astype(jnp.int32)
    return pl.pallas_call(
        local_iteration,
        out_shape=jax.ShapeDtypeStruct(values.shape, jnp.float32),
        in_specs=[smem] + [vmem] * 9,
        out_specs=vmem,
        scratch_shapes=[
            pltpu.VMEM((17 * 8 + 1, size, size), jnp.bfloat16),
            pltpu.VMEM((129, size, size), jnp.bfloat16),
            pltpu.VMEM((33, size, size), jnp.bfloat16),
            pltpu.VMEM((8, size), jnp.int32),
            pltpu.SMEM((8, size), jnp.int32),
            pltpu.SMEM((512,), jnp.int32),
            pltpu.SMEM((256,), jnp.int32),
            pltpu.SMEM((128,), jnp.int32),
            pltpu.SemaphoreType.DMA,
        ],
        compiler_params=pltpu.CompilerParams(vmem_limit_bytes=32 * 1024 * 1024),
    )(origin, line, line_there, *here, *there, mirrored)


def per_device(values, columns):
    sizes = (lax.axis_size("row"), lax.axis_size("col"), *values.shape)
    if sizes == (8, 4, 2, 2, 128, 128):
        return per_device_whole(values, columns)
    return per_device_panels(values, columns)


def solution(mesh):
    in_specs = (P("row", "col", None, None), P("row", "col"))
    out_specs = P("row", "col", None, None)
    return jax.shard_map(
        per_device, mesh=mesh, in_specs=in_specs, out_specs=out_specs, check_vma=False
    )
```
